256 devices in a mesh: elem: 64 (over z, x, core), band: 4 (over y).
Axes of the slice: x: 4, y: 4, z: 8, core: 2. Of those that a mesh axis runs over, the one named last changes fastest.
Arguments:
- sw_tau: bfloat16 [32, 224, 16384], P(None, 'band', 'elem'), may hold values from 0.0049743652 to 0.3984375
- sw_ssa: bfloat16 [32, 224, 16384], P(None, 'band', 'elem'), may hold values from 0 to 0.94921875
- lw_tau: bfloat16 [32, 224, 16384], P(None, 'band', 'elem'), may hold values from 0.0099487305 to 2
- lw_source: bfloat16 [32, 224, 16384], P(None, 'band', 'elem'), may hold values from 0.29882812 to 3
- cosine: float32 [16384], P('elem'), may hold values from 0.2 to 1
- surface_albedo: float32 [14, 16384], P(None, 'elem'), may hold values from 0.05 to 0.8
- lit_mask: int32 [16384], P('elem'), may hold values from 0 to 1, as said below
- column_map: int32 [16384], P('elem'), may hold values from 0 to 16383, as said below
- band_solar: float32 [14], replicated, may hold values from 4 to 16
- band_table: int32 [224], P('band'), may hold values from 0 to 13
Outputs:
- heating: float32 [2, 32, 16384], P(None, 'band', 'elem')
The draws below stay inside these ranges and needn't reach their ends.
Inputs may be any that keep to these rules, and one draw needn't show every extreme that they name: `column_map`: A permutation of the columns; the 256 entries of each index of elem name exactly 256 / 64 positions in the block of 256 span positions of every index of elem. `lit_mask`: index i and index i + 64 / 2 of elem (modulo 64) together hold exactly 256 lit columns; in every draw some index of elem has all its columns lit.
All inputs are finite; a program needn't handle non-finite values.
Results may differ from the reference program's by a relative error of at most 0.0035.
Values may be sent and summed in bfloat16 or wider, within the bound.
A program may use at most 128 MiB of HBM per device.

```python
import math
import jax
import jax.numpy as jnp
from jax import lax

LEV = 32
G = 224
NBND = 14
COL_DEV = 256
NCOL = 16384


def draw_column_map(key, part):
    key = jax.random.fold_in(key, 11)
    groups = NCOL // COL_DEV
    per_peer = COL_DEV // groups
    key_dest, key_mix = jax.random.split(key)
    local_idx = jnp.arange(COL_DEV, dtype=jnp.int32)
    dest_dev = local_idx // per_peer
    within_idx = local_idx % per_peer
    source_dev = jnp.arange(groups, dtype=jnp.int32)
    slot_idx = source_dev[:, None] * per_peer + within_idx[None, :]
    shuffles = jax.vmap(lambda sub: jax.random.permutation(sub, COL_DEV))(jax.random.split(key_dest, groups))
    targets = shuffles[dest_dev[None, :], slot_idx] + dest_dev[None, :] * COL_DEV
    mixing = jax.vmap(lambda sub: jax.random.permutation(sub, COL_DEV))(jax.random.split(key_mix, groups))
    shuffled = jnp.take_along_axis(targets, mixing, axis=1)
    return shuffled.reshape(NCOL).astype(jnp.int32)


def draw_lit_mask(key, part):
    key = jax.random.fold_in(key, 23)
    groups = NCOL // COL_DEV
    pair_count = groups // 2
    half_cols = COL_DEV // 2
    subkeys = jax.random.split(key, 4)
    surplus = jax.random.randint(subkeys[0], (pair_count,), 0, half_cols + 1)
    full_pair = jax.random.randint(subkeys[1], (), 0, pair_count)
    surplus = jnp.where(jnp.arange(pair_count) == full_pair, half_cols, surplus)
    heavier = half_cols + surplus
    flipped = jax.random.randint(subkeys[2], (pair_count,), 0, 2)
    lead_counts = jnp.where(flipped == 1, heavier, COL_DEV - heavier)
    counts = jnp.concatenate([lead_counts, COL_DEV - lead_counts])
    ranking = jax.vmap(lambda sub: jax.random.permutation(sub, COL_DEV))(jax.random.split(subkeys[3], groups))
    return (ranking < counts[:, None]).reshape(NCOL).astype(jnp.int32)


def place_ends(values, stream_key, least, top_value):
    longest = values.shape.index(max(values.shape))
    spots = []
    for shift in (0, 1):
        where = [jax.random.randint(jax.random.fold_in(stream_key, axis), (), 0, length) for axis, length in enumerate(values.shape)]
        where[longest] = (where[longest] + shift) % values.shape[longest]
        spots.append(tuple(where))
    return values.at[spots[0]].set(least).at[spots[1]].set(top_value)


def levels(own_key, extent, cuts, low, largest):
    gain, own = 1.0, jax.random.fold_in(own_key, 6)
    for position, blocks in cuts:
        steps = jnp.exp(jax.random.uniform(jax.random.fold_in(own, position), (blocks,), jnp.float32, low / len(cuts), largest / len(cuts)))
        gain = gain * jnp.repeat(steps, extent[position] // blocks).reshape([-1 if axis == position else 1 for axis in range(len(extent))])
    return gain


def setup_inputs(seed: int = 0) -> dict:
    streams_of = jax.random.split(jax.random.key(seed), 11)
    sw_tau = jnp.clip(jnp.exp(math.log(0.3984375) - 4.383253 * jax.random.uniform(streams_of[0], (LEV, G, NCOL), jnp.float32) ** levels(streams_of[0], (LEV, G, NCOL), ((1, 4), (2, 64)), -0.2, 0.2)), 0.0049743652, 0.3984375).astype(jnp.bfloat16)
    sw_ssa = jnp.clip(0.94921875 * jax.random.uniform(streams_of[1], (LEV, G, NCOL), jnp.float32) ** levels(streams_of[1], (LEV, G, NCOL), ((1, 4), (2, 64)), -0.2, 0.2), 0.0, 0.94921875).astype(jnp.bfloat16)
    lw_tau = jnp.clip(jnp.exp(math.log(2.0) - 5.3034575 * jax.random.uniform(streams_of[2], (LEV, G, NCOL), jnp.float32) ** levels(streams_of[2], (LEV, G, NCOL), ((1, 4), (2, 64)), -0.2, 0.2)), 0.0099487305, 2.0).astype(jnp.bfloat16)
    lw_source = jnp.clip(jnp.exp(math.log(3.0) - 2.306499 * jax.random.uniform(streams_of[3], (LEV, G, NCOL), jnp.float32) ** levels(streams_of[3], (LEV, G, NCOL), ((1, 4), (2, 64)), -0.2, 0.2)), 0.29882812, 3.0).astype(jnp.bfloat16)
    cosine = jnp.clip(0.2 + 0.8 * jax.random.uniform(streams_of[4], (NCOL,), jnp.float32) ** levels(streams_of[4], (NCOL,), ((0, 64),), -0.2, 0.2), 0.2, 1.0)
    surface_albedo = jnp.clip(0.05 + 0.75 * jax.random.uniform(streams_of[5], (NBND, NCOL), jnp.float32) ** levels(streams_of[5], (NBND, NCOL), ((1, 64),), -0.2, 0.2), 0.05, 0.8)
    lit_mask = draw_lit_mask(jax.random.fold_in(streams_of[10], 71), 0)
    column_map = draw_column_map(jax.random.fold_in(streams_of[10], 71), 0)
    band_solar = jnp.clip(jnp.exp(jax.random.uniform(streams_of[8], (NBND,), jnp.float32, math.log(4.0), math.log(16.0))), 4.0, 16.0)
    band_table = place_ends(jax.random.randint(streams_of[9], (G,), 0, NBND), jax.random.fold_in(streams_of[9], 1), 0, NBND - 1).astype(jnp.int32)
    return dict(sw_tau=sw_tau, sw_ssa=sw_ssa, lw_tau=lw_tau, lw_source=lw_source, cosine=cosine, surface_albedo=surface_albedo, lit_mask=lit_mask, column_map=column_map, band_solar=band_solar, band_table=band_table)


def affine_step(earlier, later):
    return (earlier[0] * later[0], later[0] * earlier[1] + later[1])


def shortwave(sw_depth, sw_albedo, cosine, albedo, band_solar, onehot):
    optical = sw_depth.astype(jnp.float32)
    extinct = optical * (1.0 - 0.5 * sw_albedo.astype(jnp.float32))
    zero_rows = jnp.zeros_like(optical[:1])
    depth = jnp.concatenate([zero_rows, jnp.cumsum(extinct, axis=0)], axis=0)
    incoming = jnp.dot(onehot, band_solar, precision=lax.Precision.HIGHEST)[:, None] * cosine[None, :]
    direct = incoming[None] * jnp.exp(-depth / cosine[None, None, :])
    surface = jnp.dot(onehot, albedo, precision=lax.Precision.HIGHEST)
    column_above = jnp.concatenate([jnp.cumsum(optical[::-1], axis=0)[::-1], zero_rows], axis=0)
    upward = (surface * direct[-1])[None] * jnp.exp(-1.66 * column_above)
    layer = direct[:-1] * (-jnp.expm1(-extinct / cosine[None, None, :])) + upward[1:] * (-jnp.expm1(-1.66 * optical))
    return jnp.sum(layer, axis=1)


def longwave(lw_depth, lw_planck):
    optical = lw_depth.astype(jnp.float32)
    planck = lw_planck.astype(jnp.float32)
    loss = -jnp.expm1(-1.66 * optical)
    transmit = jnp.exp(-1.66 * optical)
    emitted = planck * loss
    zero_rows = jnp.zeros_like(optical[:1])
    _, downward = lax.associative_scan(affine_step, (transmit, emitted), axis=0)
    downward = jnp.concatenate([zero_rows, downward], axis=0)
    factor, offset = lax.associative_scan(affine_step, (transmit[::-1], emitted[::-1]), axis=0)
    upper = (factor * planck[-1][None] + offset)[::-1]
    upward = jnp.concatenate([upper, planck[-1:]], axis=0)
    layer = loss * (downward[:-1] + upward[1:] - 2.0 * planck)
    return jnp.sum(layer, axis=1)


def reference(sw_tau, sw_ssa, lw_tau, lw_source, cosine, surface_albedo, lit_mask, column_map, band_solar, band_table):
    sorting = jnp.argsort(column_map)
    per_block = G // 8
    bands = jnp.arange(NBND, dtype=jnp.int32)

    def one_block(totals, g_start):
        table_part = lax.dynamic_slice_in_dim(band_table, g_start, per_block, 0)
        onehot = (table_part[:, None] == bands[None, :]).astype(jnp.float32)
        depth_part = lax.dynamic_slice_in_dim(sw_tau, g_start, per_block, 1)[:, :, sorting]
        albedo_part = lax.dynamic_slice_in_dim(sw_ssa, g_start, per_block, 1)[:, :, sorting]
        lw_part = lax.dynamic_slice_in_dim(lw_tau, g_start, per_block, 1)
        source_part = lax.dynamic_slice_in_dim(lw_source, g_start, per_block, 1)
        sw_heat = shortwave(depth_part, albedo_part, cosine, surface_albedo, band_solar, onehot)
        lw_heat = longwave(lw_part, source_part)
        return totals + jnp.stack([sw_heat, lw_heat]), None

    starts = (jnp.arange(8) * per_block).astype(jnp.int32)
    init = jnp.zeros((2, LEV, NCOL), jnp.float32)
    totals, _ = lax.scan(one_block, init, starts)
    lit = lit_mask.astype(jnp.float32)
    scaled = totals * (1.0 / G)
    return jnp.stack([scaled[0] * lit[None, :], scaled[1]])
```

```python
import functools
import math

import jax
import jax.numpy as jnp
from jax import lax
from jax.experimental import pallas as pl
from jax.experimental.pallas import tpu as pltpu
from jax.sharding import PartitionSpec as P

F = jnp.float32
B = jnp.bfloat16
LOG2E = math.log2(math.e)
DIFFUSE = -1.66 * LOG2E
Z, X, CORES, BANDS = 8, 4, 2, 4
ELEMS = Z * X * CORES
LEVELS, POINTS, COLS, ALBEDOS = 32, 56, 256, 14
SHARE = COLS // ELEMS
OUT_LEVELS = LEVELS // BANDS


def elem_offsets():
    offsets = [(a, b, c) for a in range(Z) for b in range(X) for c in range(CORES)][1:]
    return sorted(offsets, key=lambda o: -(min(o[0], Z - o[0]) + min(o[1], X - o[1])))


def iota(shape, dim):
    return lax.broadcasted_iota(jnp.int32, shape, dim)


def over_points(x):
    return jnp.sum(x.reshape(POINTS // 8, 8, x.shape[-1]), axis=0)


def pieces(x, n):
    out = []
    for _ in range(n):
        part = x.astype(B).astype(F)
        out.append(part)
        x = x - part
    return out


def spread(rows, onehot):
    tiled = jnp.concatenate([rows] * SHARE, axis=0)
    picked = jnp.dot(onehot, tiled.T.astype(B), preferred_element_type=F)
    lane_share = iota((ELEMS, 128), 1) // 32
    out = jnp.zeros((ELEMS, 128), F)
    for s in range(SHARE):
        out = jnp.where(lane_share == s, picked[s * ELEMS : (s + 1) * ELEMS], out)
    return out


def collect(received, onehot):
    turned = received.T.astype(B)
    out = jnp.zeros((32, COLS), F)
    for s in range(SHARE):
        out = out + jnp.dot(
            turned[s * 32 : (s + 1) * 32],
            onehot[s * ELEMS : (s + 1) * ELEMS],
            preferred_element_type=F,
        )
    return out


def kernel(
    sw_tau, sw_ssa, lw_tau, lw_source, cosine_h, albedo_h, lit_h, map_h, solar_h, table_h,
    out,
    cosine, albedo, lit, column_map, solar, table,
    tau_v, ssa_v, ltau_v, lsrc_v, work_a, work_b, sums, onehot_dyn, onehot_span, params,
    ask_out, ask_in, tell_out, tell_in, give_out, give_in,
    lw_out, lw_in, sw_out, sw_in,
    load_sems, send_sems, recv_sems,
):
    me, band = lax.axis_index("elem"), lax.axis_index("band")
    z, x, core = me // (X * CORES), (me // CORES) % X, me % CORES
    elem_peers = [
        (((z + a) % Z) * (X * CORES) + ((x + b) % X) * CORES + (core + c) % CORES)
        for a, b, c in elem_offsets()
    ]
    band_peers = [(band + i) % BANDS for i in (2, 1, 3)]
    mesh_ids = pl.DeviceIdType.MESH

    map_load = pltpu.make_async_copy(map_h, column_map, load_sems.at[0])
    map_load.start()
    barrier = pltpu.get_barrier_semaphore()
    for p in elem_peers:
        pl.semaphore_signal(barrier, inc=1, device_id=(p, band), device_id_type=mesh_ids)
    for p in band_peers:
        pl.semaphore_signal(barrier, inc=1, device_id=(me, p), device_id_type=mesh_ids)

    loads = [
        pltpu.make_async_copy(src, dst, load_sems.at[1 + i])
        for i, (src, dst) in enumerate(
            [
                (lw_tau, ltau_v), (lw_source, lsrc_v), (sw_tau, tau_v), (sw_ssa, ssa_v),
                (cosine_h, cosine), (albedo_h, albedo), (lit_h, lit), (solar_h, solar), (table_h, table),
            ]
        )
    ]
    for copy in loads:
        copy.start()

    def send_rows(src, dst, i):
        for p in elem_peers:
            pltpu.make_async_remote_copy(
                src_ref=src.at[p],
                dst_ref=dst.at[me],
                send_sem=send_sems.at[i],
                recv_sem=recv_sems.at[i],
                device_id=(p, band),
                device_id_type=mesh_ids,
            ).start()
        dst[pl.ds(me, 1)] = src[pl.ds(me, 1)]

    def rows_of(ref):
        return ref.at[pl.ds(0, ELEMS - 1)]

    def wait_rows(ref, i, sems):
        pltpu.make_async_copy(rows_of(ref), rows_of(ref), sems.at[i]).wait()

    def send_levels(src, dst, i):
        for p in band_peers:
            pltpu.make_async_remote_copy(
                src_ref=src.at[p],
                dst_ref=dst.at[band],
                send_sem=send_sems.at[i],
                recv_sem=recv_sems.at[i],
                device_id=(me, p),
                device_id_type=mesh_ids,
            ).start()

    def wait_levels(ref, i, sems):
        part = ref.at[pl.ds(0, BANDS - 1)]
        pltpu.make_async_copy(part, part, sems.at[i]).wait()

    def total_levels(src, dst):
        total = src[band]
        for p in band_peers:
            total = total + dst[p]
        return total

    map_load.wait()
    place = column_map[...]
    owner, slot = place >> 8, place & 255
    turned = jnp.broadcast_to(place.astype(F), (8, COLS)).T[:, 0:1].astype(jnp.int32)
    earlier = ((turned >> 8) == owner) & (iota((COLS, COLS), 0) < iota((COLS, COLS), 1))
    rank = jnp.sum(earlier.astype(F), axis=0, keepdims=True).astype(jnp.int32)
    key = owner + rank * ELEMS
    onehot_dyn[...] = (key == iota((COLS, COLS), 0)).astype(F).astype(B)
    slots = jnp.broadcast_to((turned & 255).astype(F), (COLS, 128)).astype(B)
    asked = jnp.dot(onehot_dyn[...], slots, preferred_element_type=F)
    lane = iota((ELEMS, 128), 1)
    asking = jnp.zeros((ELEMS, 128), F)
    for s in range(SHARE):
        asking = jnp.where(lane == s, asked[s * ELEMS : (s + 1) * ELEMS], asking)
    ask_out[:, 0, :] = asking

    pl.semaphore_wait(barrier, len(elem_peers) + len(band_peers))
    send_rows(ask_out, ask_in, 0)

    for copy in loads[4:]:
        copy.wait()
    high, low = pieces(albedo[...], 2)
    params[...] = jnp.zeros((32, COLS), F)
    params[0:ALBEDOS] = high
    params[16 : 16 + ALBEDOS] = low
    first, second, third = pieces(cosine[...], 3)
    params[14:15] = first
    params[15:16] = second
    params[30:31] = third

    loads[0].wait()
    loads[1].wait()

    def lw_down(k, down):
        planck = lsrc_v[k].astype(F)
        trans = jnp.exp2(ltau_v[k].astype(F) * DIFFUSE)
        emitted = planck - planck * trans
        work_a[k] = trans
        work_b[k] = emitted
        sums[k] = over_points(down)
        return trans * down + emitted

    down = lax.fori_loop(0, LEVELS, lw_down, jnp.zeros((POINTS, COLS), F), unroll=2)
    surface = lsrc_v[LEVELS - 1].astype(F)
    sums[LEVELS] = over_points(down - surface)

    def lw_up(i, up):
        k = LEVELS - 1 - i
        up = work_a[k] * up + work_b[k]
        sums[k] = sums[k] - over_points(up)
        return up

    lax.fori_loop(0, LEVELS, lw_up, surface, unroll=2)

    def layers():
        return jnp.sum(sums[0:LEVELS] - sums[1 : LEVELS + 1], axis=1)

    lw_out[...] = layers().reshape(BANDS, OUT_LEVELS, COLS)
    send_levels(lw_out, lw_in, 3)

    wait_rows(ask_in, 0, recv_sems)
    asked_of_me = ask_in[:, 0, :].astype(jnp.int32)
    position = iota((ELEMS, COLS), 1)
    for s in range(SHARE):
        onehot_span[s * ELEMS : (s + 1) * ELEMS] = (
            (asked_of_me[:, s : s + 1] == position).astype(F).astype(B)
        )
    tell_out[:, 0, :] = spread(params[...], onehot_span[...])
    send_rows(tell_out, tell_in, 1)

    loads[2].wait()
    loads[3].wait()

    def sw_before(i, carry):
        depth, above = carry
        k = LEVELS - 1 - i
        depth = depth + tau_v[i].astype(F) * (1.0 - 0.5 * ssa_v[i].astype(F))
        above = above * jnp.exp2(tau_v[k].astype(F) * DIFFUSE)
        work_a[i] = depth
        work_b[k] = above
        return depth, above

    lax.fori_loop(
        0, LEVELS, sw_before, (jnp.zeros((POINTS, COLS), F), jnp.ones((POINTS, COLS), F)), unroll=2
    )
    diagonal = iota((POINTS, POINTS), 0) == iota((POINTS, POINTS), 1)
    group = jnp.sum(
        jnp.where(diagonal, table[...].astype(F), 0.0), axis=1, keepdims=True
    ).astype(jnp.int32)
    solar_g = jnp.sum(
        jnp.where(iota((POINTS, ALBEDOS), 1) == group, solar[...], 0.0), axis=1, keepdims=True
    )
    lanes = iota((POINTS, 32), 1)
    picks = ((lanes == group) | (lanes == group + 16)).astype(F).astype(B)

    wait_rows(tell_in, 1, recv_sems)
    told = collect(tell_in[:, 0, :], onehot_dyn[...])
    cosine_d = told[14:15] + told[15:16] + told[30:31]
    albedo_g = jnp.dot(picks, told.astype(B), preferred_element_type=F)
    slant = -LOG2E / cosine_d
    top = solar_g * cosine_d
    bottom = top * jnp.exp2(work_a[LEVELS - 1] * slant)
    upward = albedo_g * bottom
    sums[0] = over_points(top - upward * work_b[0])
    sums[LEVELS] = over_points(bottom - upward)

    def sw_net(k, carry):
        sums[k] = over_points(top * jnp.exp2(work_a[k - 1] * slant) - upward * work_b[k])
        return carry

    lax.fori_loop(1, LEVELS, sw_net, 0)
    sw_out[...] = layers().reshape(BANDS, OUT_LEVELS, COLS)
    send_levels(sw_out, sw_in, 4)
    wait_levels(lw_in, 3, recv_sems)
    scale = 1.0 / (POINTS * BANDS)
    out[1] = total_levels(lw_out, lw_in) * scale

    wait_levels(sw_in, 4, recv_sems)
    total = total_levels(sw_out, sw_in) * scale
    parts = pieces(total, 3) + [jnp.zeros_like(total)]
    give_out[:, 0, :] = spread(jnp.concatenate(parts, axis=0), onehot_dyn[...])
    send_rows(give_out, give_in, 2)
    wait_rows(give_in, 2, recv_sems)
    given = collect(give_in[:, 0, :], onehot_span[...])
    heat = given[0:8] + given[8:16] + given[16:24]
    out[0] = heat * lit[...].astype(F)

    for i, ref in enumerate((ask_out, tell_out, give_out)):
        wait_rows(ref, i, send_sems)
    for i, ref in ((3, lw_out), (4, sw_out)):
        wait_levels(ref, i, send_sems)


def local(
    sw_tau, sw_ssa, lw_tau, lw_source, cosine, surface_albedo, lit_mask, column_map, band_solar, band_table
):
    optics = pltpu.VMEM((LEVELS, POINTS, COLS), B)
    work = pltpu.VMEM((LEVELS, POINTS, COLS), F)
    rows = pltpu.VMEM((ELEMS, 1, 128), F)
    levels = pltpu.VMEM((BANDS, OUT_LEVELS, COLS), F)
    in_hbm = pl.BlockSpec(memory_space=pltpu.HBM)
    in_vmem = pl.BlockSpec(memory_space=pltpu.VMEM)
    return pl.pallas_call(
        kernel,
        out_shape=jax.ShapeDtypeStruct((2, OUT_LEVELS, COLS), F),
        in_specs=[in_hbm] * 10,
        out_specs=in_vmem,
        scratch_shapes=[
            pltpu.VMEM((1, COLS), F),
            pltpu.VMEM((ALBEDOS, COLS), F),
            pltpu.VMEM((1, COLS), jnp.int32),
            pltpu.VMEM((1, COLS), jnp.int32),
            pltpu.VMEM((1, ALBEDOS), F),
            pltpu.VMEM((1, POINTS), jnp.int32),
            optics, optics, optics, optics, work, work,
            pltpu.VMEM((LEVELS + 1, 8, COLS), F),
            pltpu.VMEM((COLS, COLS), B),
            pltpu.VMEM((COLS, COLS), B),
            pltpu.VMEM((32, COLS), F),
            rows, rows, rows, rows, rows, rows,
            levels, levels, levels, levels,
            pltpu.SemaphoreType.DMA((10,)),
            pltpu.SemaphoreType.DMA((5,)),
            pltpu.SemaphoreType.DMA((5,)),
        ],
        compiler_params=pltpu.CompilerParams(
            collective_id=0, has_side_effects=True, vmem_limit_bytes=(64 * 1024 - 512) * 1024
        ),
    )(
        sw_tau, sw_ssa, lw_tau, lw_source,
        cosine.reshape(1, COLS), surface_albedo, lit_mask.reshape(1, COLS),
        column_map.reshape(1, COLS), band_solar.reshape(1, ALBEDOS), band_table.reshape(1, POINTS),
    )


def solution(mesh):
    placed = (
        P(None, "band", "elem"),
        P(None, "band", "elem"),
        P(None, "band", "elem"),
        P(None, "band", "elem"),
        P("elem"),
        P(None, "elem"),
        P("elem"),
        P("elem"),
        P(),
        P("band"),
    )
    return jax.shard_map(
        local, mesh=mesh, in_specs=placed, out_specs=P(None, "band", "elem"), check_vma=False
    )
```

```python
import functools
import math

import jax
import jax.numpy as jnp
from jax import lax
from jax.experimental import pallas as pl
from jax.experimental.pallas import tpu as pltpu
from jax.sharding import PartitionSpec as P

F = jnp.float32
B = jnp.bfloat16
LOG2E = math.log2(math.e)
DIFFUSE = -1.66 * LOG2E
Z, X, CORES, BANDS = 8, 4, 2, 4
ELEMS = Z * X * CORES
LEVELS, POINTS, COLS, ALBEDOS = 32, 56, 256, 14
SHARE = COLS // ELEMS
OUT_LEVELS = LEVELS // BANDS


def elem_offsets():
    offsets = [(a, b, c) for a in range(Z) for b in range(X) for c in range(CORES)][1:]
    return sorted(offsets, key=lambda o: -(min(o[0], Z - o[0]) + min(o[1], X - o[1])))


def iota(shape, dim):
    return lax.broadcasted_iota(jnp.int32, shape, dim)


def over_points(x):
    return jnp.sum(x.reshape(POINTS // 8, 8, x.shape[-1]), axis=0)


def pieces(x, n):
    out = []
    for _ in range(n):
        part = x.astype(B).astype(F)
        out.append(part)
        x = x - part
    return out


def spread(rows, onehot):
    tiled = jnp.concatenate([rows] * SHARE, axis=0)
    picked = jnp.dot(onehot, tiled.T.astype(B), preferred_element_type=F)
    lane_share = iota((ELEMS, 128), 1) // 32
    out = jnp.zeros((ELEMS, 128), F)
    for s in range(SHARE):
        out = jnp.where(lane_share == s, picked[s * ELEMS : (s + 1) * ELEMS], out)
    return out


def collect(received, onehot):
    turned = received.T.astype(B)
    out = jnp.zeros((32, COLS), F)
    for s in range(SHARE):
        out = out + jnp.dot(
            turned[s * 32 : (s + 1) * 32],
            onehot[s * ELEMS : (s + 1) * ELEMS],
            preferred_element_type=F,
        )
    return out


def kernel(
    sw_tau, sw_ssa, lw_tau, lw_source, cosine_h, albedo_h, lit_h, map_h, solar_h, table_h,
    out,
    cosine, albedo, lit, column_map, solar, table,
    tau_v, ssa_v, ltau_v, lsrc_v, work_a, work_b, sums, onehot_dyn, onehot_span, params,
    ask_out, ask_in, tell_out, tell_in, give_out, give_in,
    lw_out, lw_in, sw_out, sw_in,
    load_sems, send_sems, recv_sems,
):
    me, band = lax.axis_index("elem"), lax.axis_index("band")
    z, x, core = me // (X * CORES), (me // CORES) % X, me % CORES
    elem_peers = [
        (((z + a) % Z) * (X * CORES) + ((x + b) % X) * CORES + (core + c) % CORES)
        for a, b, c in elem_offsets()
    ]
    band_peers = [(band + i) % BANDS for i in (2, 1, 3)]
    mesh_ids = pl.DeviceIdType.MESH

    map_load = pltpu.make_async_copy(map_h, column_map, load_sems.at[0])
    map_load.start()
    barrier = pltpu.get_barrier_semaphore()
    for p in elem_peers:
        pl.semaphore_signal(barrier, inc=1, device_id=(p, band), device_id_type=mesh_ids)
    for p in band_peers:
        pl.semaphore_signal(barrier, inc=1, device_id=(me, p), device_id_type=mesh_ids)

    loads = [
        pltpu.make_async_copy(src, dst, load_sems.at[1 + i])
        for i, (src, dst) in enumerate(
            [
                (lw_tau, ltau_v), (lw_source, lsrc_v), (sw_tau, tau_v), (sw_ssa, ssa_v),
                (cosine_h, cosine), (albedo_h, albedo), (lit_h, lit), (solar_h, solar), (table_h, table),
            ]
        )
    ]
    for copy in loads:
        copy.start()

    def send_rows(src, dst, i):
        for p in elem_peers:
            pltpu.make_async_remote_copy(
                src_ref=src.at[p],
                dst_ref=dst.at[me],
                send_sem=send_sems.at[i],
                recv_sem=recv_sems.at[i],
                device_id=(p, band),
                device_id_type=mesh_ids,
            ).start()
        dst[pl.ds(me, 1)] = src[pl.ds(me, 1)]

    def rows_of(ref):
        return ref.at[pl.ds(0, ELEMS - 1)]

    def wait_rows(ref, i, sems):
        pltpu.make_async_copy(rows_of(ref), rows_of(ref), sems.at[i]).wait()

    def send_levels(src, dst, i):
        for p in band_peers:
            pltpu.make_async_remote_copy(
                src_ref=src.at[p],
                dst_ref=dst.at[band],
                send_sem=send_sems.at[i],
                recv_sem=recv_sems.at[i],
                device_id=(me, p),
                device_id_type=mesh_ids,
            ).start()

    def wait_levels(ref, i, sems):
        part = ref.at[pl.ds(0, BANDS - 1)]
        pltpu.make_async_copy(part, part, sems.at[i]).wait()

    def total_levels(src, dst):
        total = src[band]
        for p in band_peers:
            total = total + dst[p]
        return total

    map_load.wait()
    place = column_map[...]
    owner, slot = place >> 8, place & 255
    turned = jnp.broadcast_to(place.astype(F), (8, COLS)).T[:, 0:1].astype(jnp.int32)
    earlier = ((turned >> 8) == owner) & (iota((COLS, COLS), 0) < iota((COLS, COLS), 1))
    rank = jnp.sum(earlier.astype(F), axis=0, keepdims=True).astype(jnp.int32)
    key = owner + rank * ELEMS
    onehot_dyn[...] = (key == iota((COLS, COLS), 0)).astype(F).astype(B)
    slots = jnp.broadcast_to((turned & 255).astype(F), (COLS, 128)).astype(B)
    asked = jnp.dot(onehot_dyn[...], slots, preferred_element_type=F)
    lane = iota((ELEMS, 128), 1)
    asking = jnp.zeros((ELEMS, 128), F)
    for s in range(SHARE):
        asking = jnp.where(lane == s, asked[s * ELEMS : (s + 1) * ELEMS], asking)
    ask_out[:, 0, :] = asking

    pl.semaphore_wait(barrier, len(elem_peers) + len(band_peers))
    send_rows(ask_out, ask_in, 0)

    for copy in loads[4:]:
        copy.wait()
    high, low = pieces(albedo[...], 2)
    params[...] = jnp.zeros((32, COLS), F)
    params[0:ALBEDOS] = high
    params[16 : 16 + ALBEDOS] = low
    first, second, third = pieces(cosine[...], 3)
    params[14:15] = first
    params[15:16] = second
    params[30:31] = third

    loads[0].wait()
    loads[1].wait()

    def lw_down(k, down):
        planck = lsrc_v[k].astype(F)
        trans = jnp.exp2(ltau_v[k].astype(F) * DIFFUSE)
        emitted = planck - planck * trans
        work_a[k] = trans
        work_b[k] = emitted
        sums[k] = over_points(down)
        return trans * down + emitted

    down = lax.fori_loop(0, LEVELS, lw_down, jnp.zeros((POINTS, COLS), F), unroll=2)
    surface = lsrc_v[LEVELS - 1].astype(F)
    sums[LEVELS] = over_points(down - surface)

    def lw_up(i, up):
        k = LEVELS - 1 - i
        up = work_a[k] * up + work_b[k]
        sums[k] = sums[k] - over_points(up)
        return up

    lax.fori_loop(0, LEVELS, lw_up, surface, unroll=2)

    def layers():
        return jnp.sum(sums[0:LEVELS] - sums[1 : LEVELS + 1], axis=1)

    lw_out[...] = layers().reshape(BANDS, OUT_LEVELS, COLS)
    send_levels(lw_out, lw_in, 3)

    wait_rows(ask_in, 0, recv_sems)
    asked_of_me = ask_in[:, 0, :].astype(jnp.int32)
    position = iota((ELEMS, COLS), 1)
    for s in range(SHARE):
        onehot_span[s * ELEMS : (s + 1) * ELEMS] = (
            (asked_of_me[:, s : s + 1] == position).astype(F).astype(B)
        )
    tell_out[:, 0, :] = spread(params[...], onehot_span[...])
    send_rows(tell_out, tell_in, 1)

    loads[2].wait()
    loads[3].wait()

    def sw_before(i, carry):
        depth, above = carry
        k = LEVELS - 1 - i
        depth = depth + tau_v[i].astype(F) * (1.0 - 0.5 * ssa_v[i].astype(F))
        above = above * jnp.exp2(tau_v[k].astype(F) * DIFFUSE)
        work_a[i] = depth
        work_b[k] = above
        return depth, above

    lax.fori_loop(
        0, LEVELS, sw_before, (jnp.zeros((POINTS, COLS), F), jnp.ones((POINTS, COLS), F)), unroll=2
    )
    diagonal = iota((POINTS, POINTS), 0) == iota((POINTS, POINTS), 1)
    group = jnp.sum(
        jnp.where(diagonal, table[...].astype(F), 0.0), axis=1, keepdims=True
    ).astype(jnp.int32)
    solar_g = jnp.sum(
        jnp.where(iota((POINTS, ALBEDOS), 1) == group, solar[...], 0.0), axis=1, keepdims=True
    )
    lanes = iota((POINTS, 32), 1)
    picks = ((lanes == group) | (lanes == group + 16)).astype(F).astype(B)

    wait_rows(tell_in, 1, recv_sems)
    told = collect(tell_in[:, 0, :], onehot_dyn[...])
    cosine_d = told[14:15] + told[15:16] + told[30:31]
    albedo_g = jnp.dot(picks, told.astype(B), preferred_element_type=F)
    slant = -LOG2E / cosine_d
    top = solar_g * cosine_d
    bottom = top * jnp.exp2(work_a[LEVELS - 1] * slant)
    upward = albedo_g * bottom
    sums[0] = over_points(top - upward * work_b[0])
    sums[LEVELS] = over_points(bottom - upward)

    def sw_net(k, carry):
        sums[k] = over_points(top * jnp.exp2(work_a[k - 1] * slant) - upward * work_b[k])
        return carry

    lax.fori_loop(1, LEVELS, sw_net, 0)
    sw_out[...] = layers().reshape(BANDS, OUT_LEVELS, COLS)
    send_levels(sw_out, sw_in, 4)
    wait_levels(lw_in, 3, recv_sems)
    scale = 1.0 / (POINTS * BANDS)
    out[1] = total_levels(lw_out, lw_in) * scale

    wait_levels(sw_in, 4, recv_sems)
    total = total_levels(sw_out, sw_in) * scale
    parts = pieces(total, 3) + [jnp.zeros_like(total)]
    give_out[:, 0, :] = spread(jnp.concatenate(parts, axis=0), onehot_dyn[...])
    send_rows(give_out, give_in, 2)
    wait_rows(give_in, 2, recv_sems)
    given = collect(give_in[:, 0, :], onehot_span[...])
    heat = given[0:8] + given[8:16] + given[16:24]
    out[0] = heat * lit[...].astype(F)

    for i, ref in enumerate((ask_out, tell_out, give_out)):
        wait_rows(ref, i, send_sems)
    for i, ref in ((3, lw_out), (4, sw_out)):
        wait_levels(ref, i, send_sems)


def local(
    sw_tau, sw_ssa, lw_tau, lw_source, cosine, surface_albedo, lit_mask, column_map, band_solar, band_table
):
    optics = pltpu.VMEM((LEVELS, POINTS, COLS), B)
    work = pltpu.VMEM((LEVELS, POINTS, COLS), F)
    rows = pltpu.VMEM((ELEMS, 1, 128), F)
    levels = pltpu.VMEM((BANDS, OUT_LEVELS, COLS), F)
    in_hbm = pl.BlockSpec(memory_space=pltpu.HBM)
    in_vmem = pl.BlockSpec(memory_space=pltpu.VMEM)
    return pl.pallas_call(
        kernel,
        out_shape=pltpu.VMEM((2, OUT_LEVELS, COLS), F),
        in_specs=[in_hbm] * 10,
        out_specs=in_vmem,
        scratch_shapes=[
            pltpu.VMEM((1, COLS), F),
            pltpu.VMEM((ALBEDOS, COLS), F),
            pltpu.VMEM((1, COLS), jnp.int32),
            pltpu.VMEM((1, COLS), jnp.int32),
            pltpu.VMEM((1, ALBEDOS), F),
            pltpu.VMEM((1, POINTS), jnp.int32),
            optics, optics, optics, optics, work, work,
            pltpu.VMEM((LEVELS + 1, 8, COLS), F),
            pltpu.VMEM((COLS, COLS), B),
            pltpu.VMEM((COLS, COLS), B),
            pltpu.VMEM((32, COLS), F),
            rows, rows, rows, rows, rows, rows,
            levels, levels, levels, levels,
            pltpu.SemaphoreType.DMA((10,)),
            pltpu.SemaphoreType.DMA((5,)),
            pltpu.SemaphoreType.DMA((5,)),
        ],
        compiler_params=pltpu.CompilerParams(
            collective_id=0, has_side_effects=True, vmem_limit_bytes=(64 * 1024 - 512) * 1024
        ),
    )(
        sw_tau, sw_ssa, lw_tau, lw_source,
        cosine.reshape(1, COLS), surface_albedo, lit_mask.reshape(1, COLS),
        column_map.reshape(1, COLS), band_solar.reshape(1, ALBEDOS), band_table.reshape(1, POINTS),
    )


def solution(mesh):
    placed = (
        P(None, "band", "elem"),
        P(None, "band", "elem"),
        P(None, "band", "elem"),
        P(None, "band", "elem"),
        P("elem"),
        P(None, "elem"),
        P("elem"),
        P("elem"),
        P(),
        P("band"),
    )
    return jax.shard_map(
        local, mesh=mesh, in_specs=placed, out_specs=P(None, "band", "elem"), check_vma=False
    )
```

```python
import functools
import math

import jax
import jax.numpy as jnp
from jax import lax
from jax.experimental import pallas as pl
from jax.experimental.pallas import tpu as pltpu
from jax.sharding import PartitionSpec as P

F = jnp.float32
B = jnp.bfloat16
LOG2E = math.log2(math.e)
DIFFUSE = -1.66 * LOG2E
Z, X, CORES, BANDS = 8, 4, 2, 4
ELEMS = Z * X * CORES
LEVELS, POINTS, COLS, ALBEDOS = 32, 56, 256, 14
SHARE = COLS // ELEMS
OUT_LEVELS = LEVELS // BANDS


def elem_offsets():
    offsets = [(a, b, c) for a in range(Z) for b in range(X) for c in range(CORES)][1:]
    return sorted(offsets, key=lambda o: -(min(o[0], Z - o[0]) + min(o[1], X - o[1])))


def all_offsets():
    offsets = [
        (a, b, c, y) for a in range(Z) for b in range(X) for c in range(CORES) for y in range(BANDS)
    ][1:]
    return sorted(
        offsets, key=lambda o: -(min(o[0], Z - o[0]) + min(o[1], X - o[1]) + min(o[3], BANDS - o[3]))
    )


def iota(shape, dim):
    return lax.broadcasted_iota(jnp.int32, shape, dim)


def over_points(x):
    return jnp.sum(x.reshape(POINTS // 8, 8, x.shape[-1]), axis=0)


def pieces(x, n):
    out = []
    for _ in range(n):
        part = x.astype(B).astype(F)
        out.append(part)
        x = x - part
    return out


def spread(parts, onehot):
    picked = jnp.zeros((COLS, 128), F)
    for rows in parts:
        tiled = jnp.concatenate([rows] * SHARE, axis=0)
        picked = picked + jnp.dot(onehot, tiled.T.astype(B), preferred_element_type=F)
    lane_share = iota((ELEMS, 128), 1) // 32
    out = jnp.zeros((ELEMS, 128), F)
    for s in range(SHARE):
        out = jnp.where(lane_share == s, picked[s * ELEMS : (s + 1) * ELEMS], out)
    return out


def collect(received, onehot):
    turned = received.T.astype(B)
    out = jnp.zeros((32, COLS), F)
    for s in range(SHARE):
        out = out + jnp.dot(
            turned[s * 32 : (s + 1) * 32],
            onehot[s * ELEMS : (s + 1) * ELEMS],
            preferred_element_type=F,
        )
    return out


def kernel(
    sw_tau, sw_ssa, lw_tau, lw_source, cosine_h, albedo_h, lit_h, map_h, solar_h, table_h,
    out,
    cosine, albedo, lit, column_map, solar, table,
    tau_v, ssa_v, ltau_v, lsrc_v, work_a, work_b, sums, onehot_dyn, onehot_span, params,
    ask_out, ask_in, tell_out, tell_in, give_out, give_in,
    lw_out, lw_in, mine,
    load_sems, send_sems, recv_sems,
):
    me, band = lax.axis_index("elem"), lax.axis_index("band")
    z, x, core = me // (X * CORES), (me // CORES) % X, me % CORES
    elem_peers = [
        (((z + a) % Z) * (X * CORES) + ((x + b) % X) * CORES + (core + c) % CORES)
        for a, b, c in elem_offsets()
    ]
    band_peers = [(band + i) % BANDS for i in (2, 1, 3)]
    mesh_ids = pl.DeviceIdType.MESH

    map_load = pltpu.make_async_copy(map_h, column_map, load_sems.at[0])
    map_load.start()
    barrier = pltpu.get_barrier_semaphore()
    for p in elem_peers:
        pl.semaphore_signal(barrier, inc=1, device_id=(p, band), device_id_type=mesh_ids)
    for p in band_peers:
        pl.semaphore_signal(barrier, inc=1, device_id=(me, p), device_id_type=mesh_ids)

    loads = [
        pltpu.make_async_copy(src, dst, load_sems.at[1 + i])
        for i, (src, dst) in enumerate(
            [
                (lw_tau, ltau_v), (lw_source, lsrc_v), (sw_tau, tau_v), (sw_ssa, ssa_v),
                (cosine_h, cosine), (albedo_h, albedo), (lit_h, lit), (solar_h, solar), (table_h, table),
            ]
        )
    ]
    for copy in loads:
        copy.start()

    def send_rows(src, dst, i):
        for p in elem_peers:
            pltpu.make_async_remote_copy(
                src_ref=src.at[p],
                dst_ref=dst.at[me],
                send_sem=send_sems.at[i],
                recv_sem=recv_sems.at[i],
                device_id=(p, band),
                device_id_type=mesh_ids,
            ).start()
        dst[pl.ds(me, 1)] = src[pl.ds(me, 1)]

    def rows_of(ref):
        return ref.at[pl.ds(0, ELEMS - 1)]

    def wait_rows(ref, i, sems):
        pltpu.make_async_copy(rows_of(ref), rows_of(ref), sems.at[i]).wait()

    def send_levels(src, dst, i):
        for p in band_peers:
            pltpu.make_async_remote_copy(
                src_ref=src.at[p],
                dst_ref=dst.at[band],
                send_sem=send_sems.at[i],
                recv_sem=recv_sems.at[i],
                device_id=(me, p),
                device_id_type=mesh_ids,
            ).start()

    def wait_levels(ref, i, sems):
        part = ref.at[pl.ds(0, BANDS - 1)]
        pltpu.make_async_copy(part, part, sems.at[i]).wait()

    def total_levels(src, dst):
        total = src[band]
        for p in band_peers:
            total = total + dst[p]
        return total

    map_load.wait()
    place = column_map[...]
    owner, slot = place >> 8, place & 255
    turned = jnp.broadcast_to(place.astype(F), (8, COLS)).T[:, 0:1].astype(jnp.int32)
    earlier = ((turned >> 8) == owner) & (iota((COLS, COLS), 0) < iota((COLS, COLS), 1))
    rank = jnp.sum(earlier.astype(F), axis=0, keepdims=True).astype(jnp.int32)
    key = owner + rank * ELEMS
    onehot_dyn[...] = (key == iota((COLS, COLS), 0)).astype(F).astype(B)
    slots = jnp.broadcast_to((turned & 255).astype(F), (COLS, 128)).astype(B)
    asked = jnp.dot(onehot_dyn[...], slots, preferred_element_type=F)
    lane = iota((ELEMS, 128), 1)
    asking = jnp.zeros((ELEMS, 128), F)
    for s in range(SHARE):
        asking = jnp.where(lane == s, asked[s * ELEMS : (s + 1) * ELEMS], asking)
    ask_out[:, 0, :] = asking

    pl.semaphore_wait(barrier, len(elem_peers) + len(band_peers))
    send_rows(ask_out, ask_in, 0)

    for copy in loads[4:]:
        copy.wait()
    high, low = pieces(albedo[...], 2)
    params[...] = jnp.zeros((32, COLS), F)
    params[0:ALBEDOS] = high
    params[16 : 16 + ALBEDOS] = low
    first, second, third = pieces(cosine[...], 3)
    params[14:15] = first
    params[15:16] = second
    params[30:31] = third

    loads[0].wait()
    loads[1].wait()

    def lw_down(k, down):
        planck = lsrc_v[k].astype(F)
        trans = jnp.exp2(ltau_v[k].astype(F) * DIFFUSE)
        emitted = planck - planck * trans
        work_a[k] = trans
        work_b[k] = emitted
        sums[k] = over_points(down)
        return trans * down + emitted

    down = lax.fori_loop(0, LEVELS, lw_down, jnp.zeros((POINTS, COLS), F), unroll=2)
    surface = lsrc_v[LEVELS - 1].astype(F)
    sums[LEVELS] = over_points(down - surface)

    def lw_up(i, up):
        k = LEVELS - 1 - i
        up = work_a[k] * up + work_b[k]
        sums[k] = sums[k] - over_points(up)
        return up

    lax.fori_loop(0, LEVELS, lw_up, surface, unroll=2)

    def layers():
        return jnp.sum(sums[0:LEVELS] - sums[1 : LEVELS + 1], axis=1)

    lw_out[...] = layers().reshape(BANDS, OUT_LEVELS, COLS)
    send_levels(lw_out, lw_in, 3)

    wait_rows(ask_in, 0, recv_sems)
    asked_of_me = ask_in[:, 0, :].astype(jnp.int32)
    position = iota((ELEMS, COLS), 1)
    for s in range(SHARE):
        onehot_span[s * ELEMS : (s + 1) * ELEMS] = (
            (asked_of_me[:, s : s + 1] == position).astype(F).astype(B)
        )
    tell_out[:, 0, :] = spread([params[...]], onehot_span[...])
    send_rows(tell_out, tell_in, 1)

    loads[2].wait()
    loads[3].wait()

    def sw_before(i, carry):
        depth, above = carry
        k = LEVELS - 1 - i
        depth = depth + tau_v[i].astype(F) * (1.0 - 0.5 * ssa_v[i].astype(F))
        above = above * jnp.exp2(tau_v[k].astype(F) * DIFFUSE)
        work_a[i] = depth
        work_b[k] = above
        return depth, above

    lax.fori_loop(
        0, LEVELS, sw_before, (jnp.zeros((POINTS, COLS), F), jnp.ones((POINTS, COLS), F)), unroll=2
    )
    diagonal = iota((POINTS, POINTS), 0) == iota((POINTS, POINTS), 1)
    group = jnp.sum(
        jnp.where(diagonal, table[...].astype(F), 0.0), axis=1, keepdims=True
    ).astype(jnp.int32)
    solar_g = jnp.sum(
        jnp.where(iota((POINTS, ALBEDOS), 1) == group, solar[...], 0.0), axis=1, keepdims=True
    )
    lanes = iota((POINTS, 32), 1)
    picks = ((lanes == group) | (lanes == group + 16)).astype(F).astype(B)

    wait_rows(tell_in, 1, recv_sems)
    told = collect(tell_in[:, 0, :], onehot_dyn[...])
    cosine_d = told[14:15] + told[15:16] + told[30:31]
    albedo_g = jnp.dot(picks, told.astype(B), preferred_element_type=F)
    slant = -LOG2E / cosine_d
    top = solar_g * cosine_d
    bottom = top * jnp.exp2(work_a[LEVELS - 1] * slant)
    upward = albedo_g * bottom
    sums[0] = over_points(top - upward * work_b[0])
    sums[LEVELS] = over_points(bottom - upward)

    def sw_net(k, carry):
        sums[k] = over_points(top * jnp.exp2(work_a[k - 1] * slant) - upward * work_b[k])
        return carry

    lax.fori_loop(1, LEVELS, sw_net, 0)
    give_out[:, 0, :] = spread(pieces(layers(), 2), onehot_dyn[...])
    for a, b, c, y in all_offsets():
        to = ((z + a) % Z) * (X * CORES) + ((x + b) % X) * CORES + (core + c) % CORES
        pltpu.make_async_remote_copy(
            src_ref=give_out.at[to],
            dst_ref=give_in.at[band * ELEMS + me],
            send_sem=send_sems.at[2],
            recv_sem=recv_sems.at[2],
            device_id=(to, (band + y) % BANDS),
            device_id_type=mesh_ids,
        ).start()
    give_in[pl.ds(band * ELEMS + me, 1)] = give_out[pl.ds(me, 1)]
    wait_levels(lw_in, 3, recv_sems)
    scale = 1.0 / (POINTS * BANDS)
    out[1] = total_levels(lw_out, lw_in) * scale

    all_rows = give_in.at[pl.ds(0, BANDS * ELEMS - 1)]
    pltpu.make_async_copy(all_rows, all_rows, recv_sems.at[2]).wait()
    given = give_in[:, 0, :].reshape(BANDS, ELEMS, 128)
    mine[...] = jnp.sum(given, axis=0).T.reshape(SHARE, BANDS, OUT_LEVELS, ELEMS)
    heat = jnp.zeros((2 * OUT_LEVELS, COLS), F)
    for s in range(SHARE):
        heat = heat + jnp.dot(
            jnp.concatenate(pieces(mine[s, band], 2), axis=0).astype(B),
            onehot_span[s * ELEMS : (s + 1) * ELEMS],
            preferred_element_type=F,
        )
    heat = (heat[0:OUT_LEVELS] + heat[OUT_LEVELS:]) * scale
    out[0] = heat * lit[...].astype(F)

    for i, ref in enumerate((ask_out, tell_out)):
        wait_rows(ref, i, send_sems)
    pltpu.make_async_copy(all_rows, all_rows, send_sems.at[2]).wait()
    wait_levels(lw_out, 3, send_sems)


def local(
    sw_tau, sw_ssa, lw_tau, lw_source, cosine, surface_albedo, lit_mask, column_map, band_solar, band_table
):
    optics = pltpu.VMEM((LEVELS, POINTS, COLS), B)
    work = pltpu.VMEM((LEVELS, POINTS, COLS), F)
    rows = pltpu.VMEM((ELEMS, 1, 128), F)
    levels = pltpu.VMEM((BANDS, OUT_LEVELS, COLS), F)
    in_hbm = pl.BlockSpec(memory_space=pltpu.HBM)
    in_vmem = pl.BlockSpec(memory_space=pltpu.VMEM)
    return pl.pallas_call(
        kernel,
        out_shape=pltpu.VMEM((2, OUT_LEVELS, COLS), F),
        in_specs=[in_hbm] * 10,
        out_specs=in_vmem,
        scratch_shapes=[
            pltpu.VMEM((1, COLS), F),
            pltpu.VMEM((ALBEDOS, COLS), F),
            pltpu.VMEM((1, COLS), jnp.int32),
            pltpu.VMEM((1, COLS), jnp.int32),
            pltpu.VMEM((1, ALBEDOS), F),
            pltpu.VMEM((1, POINTS), jnp.int32),
            optics, optics, optics, optics, work, work,
            pltpu.VMEM((LEVELS + 1, 8, COLS), F),
            pltpu.VMEM((COLS, COLS), B),
            pltpu.VMEM((COLS, COLS), B),
            pltpu.VMEM((32, COLS), F),
            rows, rows, rows, rows, rows,
            pltpu.VMEM((BANDS * ELEMS, 1, 128), F),
            levels, levels,
            pltpu.VMEM((SHARE, BANDS, OUT_LEVELS, ELEMS), F),
            pltpu.SemaphoreType.DMA((10,)),
            pltpu.SemaphoreType.DMA((4,)),
            pltpu.SemaphoreType.DMA((4,)),
        ],
        compiler_params=pltpu.CompilerParams(
            collective_id=0, has_side_effects=True, vmem_limit_bytes=(64 * 1024 - 512) * 1024
        ),
    )(
        sw_tau, sw_ssa, lw_tau, lw_source,
        cosine.reshape(1, COLS), surface_albedo, lit_mask.reshape(1, COLS),
        column_map.reshape(1, COLS), band_solar.reshape(1, ALBEDOS), band_table.reshape(1, POINTS),
    )


def solution(mesh):
    placed = (
        P(None, "band", "elem"),
        P(None, "band", "elem"),
        P(None, "band", "elem"),
        P(None, "band", "elem"),
        P("elem"),
        P(None, "elem"),
        P("elem"),
        P("elem"),
        P(),
        P("band"),
    )
    return jax.shard_map(
        local, mesh=mesh, in_specs=placed, out_specs=P(None, "band", "elem"), check_vma=False
    )
```

```python
import functools
import math

import jax
import jax.numpy as jnp
from jax import lax
from jax.experimental import pallas as pl
from jax.experimental.pallas import tpu as pltpu
from jax.sharding import PartitionSpec as P

F = jnp.float32
B = jnp.bfloat16
LOG2E = math.log2(math.e)
DIFFUSE = -1.66 * LOG2E
Z, X, CORES, BANDS = 8, 4, 2, 4
ELEMS = Z * X * CORES
LEVELS, POINTS, COLS, ALBEDOS = 32, 56, 256, 14
SHARE = COLS // ELEMS
OUT_LEVELS = LEVELS // BANDS
NEAR = 4


def elem_offsets():
    offsets = [(a, b, c) for a in range(Z) for b in range(X) for c in range(CORES)][1:]
    return sorted(offsets, key=lambda o: -(min(o[0], Z - o[0]) + min(o[1], X - o[1])))


def far_offsets():
    return [o for o in elem_offsets() if min(o[0], Z - o[0]) + min(o[1], X - o[1]) > NEAR]


def all_offsets():
    offsets = [
        (a, b, c, y) for a in range(Z) for b in range(X) for c in range(CORES) for y in range(BANDS)
    ][1:]
    return sorted(
        offsets, key=lambda o: -(min(o[0], Z - o[0]) + min(o[1], X - o[1]) + min(o[3], BANDS - o[3]))
    )


def iota(shape, dim):
    return lax.broadcasted_iota(jnp.int32, shape, dim)


def over_points(x):
    return jnp.sum(x.reshape(POINTS // 8, 8, x.shape[-1]), axis=0)


def pieces(x, n):
    out = []
    for _ in range(n):
        part = x.astype(B).astype(F)
        out.append(part)
        x = x - part
    return out


def tiled(rows):
    return jnp.concatenate([rows.astype(B)] * SHARE, axis=0)


def spread(parts, onehot):
    picked = [
        lax.dot_general(onehot, rows, (((1,), (1,)), ((), ())), preferred_element_type=F)
        for rows in parts
    ]
    picked = functools.reduce(jnp.add, picked)
    lane_share = iota((ELEMS, 128), 1) // 32
    out = picked[:ELEMS]
    for s in range(1, SHARE):
        out = jnp.where(lane_share == s, picked[s * ELEMS : (s + 1) * ELEMS], out)
    return out


def collect(received, onehot):
    turned = received.T.astype(B)
    out = jnp.zeros((32, COLS), F)
    for s in range(SHARE):
        out = out + jnp.dot(
            turned[s * 32 : (s + 1) * 32],
            onehot[s * ELEMS : (s + 1) * ELEMS],
            preferred_element_type=F,
        )
    return out


def kernel(
    sw_tau, sw_ssa, lw_tau, lw_source, cosine_h, albedo_h, lit_h, map_h, solar_h, table_h,
    out,
    cosine, albedo, lit, column_map, solar, table,
    tau_v, ssa_v, ltau_v, lsrc_v, work_a, work_b, sums, onehot_dyn, onehot_span, params,
    ask_out, ask_in, tell_out, tell_in, give_out, give_in,
    lw_out, lw_in, mine, telling, ask_far, push_out, push_in, slot_of,
    load_sems, send_sems, recv_sems,
):
    me, band = lax.axis_index("elem"), lax.axis_index("band")
    z, x, core = me // (X * CORES), (me // CORES) % X, me % CORES


    def at(a, b, c):
        return ((z + a) % Z) * (X * CORES) + ((x + b) % X) * CORES + (core + c) % CORES

    far = far_offsets()
    far_peers = [at(*o) for o in far]
    near_peers = [at(*o) for o in elem_offsets() if o not in far]
    elem_peers = far_peers + near_peers
    band_peers = [(band + i) % BANDS for i in (2, 1, 3)]
    mesh_ids = pl.DeviceIdType.MESH

    map_load = pltpu.make_async_copy(map_h, column_map, load_sems.at[0])
    map_load.start()
    barrier = pltpu.get_barrier_semaphore()
    for p in elem_peers:
        pl.semaphore_signal(barrier, inc=1, device_id=(p, band), device_id_type=mesh_ids)
    for p in band_peers:
        pl.semaphore_signal(barrier, inc=1, device_id=(me, p), device_id_type=mesh_ids)

    loads = [
        pltpu.make_async_copy(src, dst, load_sems.at[1 + i])
        for i, (src, dst) in enumerate(
            [
                (lw_tau, ltau_v), (lw_source, lsrc_v), (sw_tau, tau_v), (sw_ssa, ssa_v),
                (cosine_h, cosine), (albedo_h, albedo), (lit_h, lit), (solar_h, solar), (table_h, table),
            ]
        )
    ]
    for copy in loads:
        copy.start()

    def send_rows(src, dst, i, peers):
        for p in peers:
            pltpu.make_async_remote_copy(
                src_ref=src.at[p],
                dst_ref=dst.at[me],
                send_sem=send_sems.at[i],
                recv_sem=recv_sems.at[i],
                device_id=(p, band),
                device_id_type=mesh_ids,
            ).start()

    def wait_rows(ref, i, sems, peers):
        rows = ref.at[pl.ds(0, len(peers))]
        pltpu.make_async_copy(rows, rows, sems.at[i]).wait()

    def own_row(src, dst):
        dst[pl.ds(me, 1)] = src[pl.ds(me, 1)]

    def send_levels(src, dst, i):
        for p in band_peers:
            pltpu.make_async_remote_copy(
                src_ref=src.at[p],
                dst_ref=dst.at[band],
                send_sem=send_sems.at[i],
                recv_sem=recv_sems.at[i],
                device_id=(me, p),
                device_id_type=mesh_ids,
            ).start()

    def wait_levels(ref, i, sems):
        part = ref.at[pl.ds(0, BANDS - 1)]
        pltpu.make_async_copy(part, part, sems.at[i]).wait()

    def total_levels(src, dst):
        total = src[band]
        for p in band_peers:
            total = total + dst[p]
        return total

    map_load.wait()
    place = column_map[...]
    owner, slot = place >> 8, place & 255
    turned = jnp.broadcast_to(place.astype(F), (8, COLS)).T[:, 0:1].astype(jnp.int32)
    earlier = ((turned >> 8) == owner) & (iota((COLS, COLS), 0) < iota((COLS, COLS), 1))
    rank = jnp.sum(earlier.astype(F), axis=0, keepdims=True).astype(jnp.int32)
    key = owner + rank * ELEMS
    onehot_dyn[...] = (key == iota((COLS, COLS), 0)).astype(F).astype(B)
    slots = jnp.broadcast_to((turned & 255).astype(F), (COLS, 128)).astype(B)
    asked = jnp.dot(onehot_dyn[...], slots, preferred_element_type=F)
    lane = iota((ELEMS, 128), 1)
    asking = jnp.zeros((ELEMS, 128), F)
    for s in range(SHARE):
        asking = jnp.where(lane == s, asked[s * ELEMS : (s + 1) * ELEMS], asking)
    ask_out[:, 0, :] = asking

    pl.semaphore_wait(barrier, len(elem_peers) + len(band_peers))
    send_rows(ask_out, ask_in, 0, near_peers)

    for copy in loads[4:]:
        copy.wait()
    high, low = pieces(albedo[...], 2)
    params[...] = jnp.zeros((32, COLS), F)
    params[0:ALBEDOS] = high
    params[16 : 16 + ALBEDOS] = low
    first, second, third = pieces(cosine[...], 3)
    params[14:15] = first
    params[15:16] = second
    params[30:31] = third
    telling[...] = tiled(params[...])
    push_out[...] = params[0:16].astype(B)
    slot_of[...] = (slot == iota((COLS, COLS), 0)).astype(F).astype(B)

    for f, (a, b, c) in enumerate(far):
        pltpu.make_async_remote_copy(
            src_ref=push_out,
            dst_ref=push_in.at[far.index(((Z - a) % Z, (X - b) % X, c))],
            send_sem=send_sems.at[4],
            recv_sem=recv_sems.at[4],
            device_id=(far_peers[f], band),
            device_id_type=mesh_ids,
        ).start()
    send_rows(ask_out, ask_far, 5, far_peers)
    own_row(ask_out, ask_in)

    loads[0].wait()
    loads[1].wait()

    def lw_down(k, down):
        planck = lsrc_v[k].astype(F)
        trans = jnp.exp2(ltau_v[k].astype(F) * DIFFUSE)
        emitted = planck - planck * trans
        work_a[k] = trans
        work_b[k] = emitted
        sums[k] = over_points(down)
        return trans * down + emitted

    down = lax.fori_loop(0, LEVELS, lw_down, jnp.zeros((POINTS, COLS), F), unroll=2)
    surface = lsrc_v[LEVELS - 1].astype(F)
    sums[LEVELS] = over_points(down - surface)

    def lw_up(i, up):
        k = LEVELS - 1 - i
        up = work_a[k] * up + work_b[k]
        sums[k] = sums[k] - over_points(up)
        return up

    lax.fori_loop(0, LEVELS, lw_up, surface, unroll=2)

    def layers():
        return jnp.sum(sums[0:LEVELS] - sums[1 : LEVELS + 1], axis=1)

    lw_out[...] = layers().reshape(BANDS, OUT_LEVELS, COLS)
    send_levels(lw_out, lw_in, 3)

    row = iota((ELEMS, 128), 0)
    apart_z, apart_x = ((row >> 3) - z) & (Z - 1), ((row >> 1) - x) & (X - 1)
    near = jnp.minimum(apart_z, Z - apart_z) + jnp.minimum(apart_x, X - apart_x) <= NEAR

    def find_span(asked_of_me):
        asked_of_me = asked_of_me.astype(jnp.int32)
        position = iota((ELEMS, COLS), 1)
        for s in range(SHARE):
            onehot_span[s * ELEMS : (s + 1) * ELEMS] = (
                (asked_of_me[:, s : s + 1] == position).astype(F).astype(B)
            )

    wait_rows(ask_in, 0, recv_sems, near_peers)
    find_span(jnp.where(near, ask_in[:, 0, :], -1.0))
    tell_out[:, 0, :] = spread([telling[...]], onehot_span[...])
    send_rows(tell_out, tell_in, 1, near_peers)
    own_row(tell_out, tell_in)

    loads[2].wait()
    loads[3].wait()

    def sw_before(i, carry):
        depth, above = carry
        k = LEVELS - 1 - i
        depth = depth + tau_v[i].astype(F) * (1.0 - 0.5 * ssa_v[i].astype(F))
        above = above * jnp.exp2(tau_v[k].astype(F) * DIFFUSE)
        work_a[i] = depth
        work_b[k] = above
        return depth, above

    lax.fori_loop(
        0, LEVELS, sw_before, (jnp.zeros((POINTS, COLS), F), jnp.ones((POINTS, COLS), F)), unroll=2
    )
    diagonal = iota((POINTS, POINTS), 0) == iota((POINTS, POINTS), 1)
    group = jnp.sum(
        jnp.where(diagonal, table[...].astype(F), 0.0), axis=1, keepdims=True
    ).astype(jnp.int32)
    solar_g = jnp.sum(
        jnp.where(iota((POINTS, ALBEDOS), 1) == group, solar[...], 0.0), axis=1, keepdims=True
    )
    lanes = iota((POINTS, 32), 1)
    picks = ((lanes == group) | (lanes == group + 16)).astype(F).astype(B)

    pltpu.make_async_copy(push_in, push_in, recv_sems.at[4]).wait()
    pushed = jnp.dot(
        push_in[...].reshape(len(far) * 16, COLS), slot_of[...], preferred_element_type=F
    ).reshape(len(far), 16, COLS)
    from_far = jnp.zeros((16, COLS), F)
    for f, p in enumerate(far_peers):
        from_far = jnp.where(owner == p, pushed[f], from_far)

    wait_rows(tell_in, 1, recv_sems, near_peers)
    told = collect(jnp.where(near, tell_in[:, 0, :], 0.0), onehot_dyn[...])
    told = jnp.concatenate([told[0:16] + from_far, told[16:32]], axis=0)
    cosine_d = told[14:15] + told[15:16] + told[30:31]
    albedo_g = jnp.dot(picks, told.astype(B), preferred_element_type=F)
    slant = -LOG2E / cosine_d
    top = solar_g * cosine_d
    bottom = top * jnp.exp2(work_a[LEVELS - 1] * slant)
    upward = albedo_g * bottom
    sums[0] = over_points(top - upward * work_b[0])
    sums[LEVELS] = over_points(bottom - upward)

    def sw_net(k, carry):
        sums[k] = over_points(top * jnp.exp2(work_a[k - 1] * slant) - upward * work_b[k])
        return carry

    lax.fori_loop(1, LEVELS, sw_net, 0, unroll=31)
    give_out[:, 0, :] = spread([tiled(p) for p in pieces(layers(), 2)], onehot_dyn[...])
    for a, b, c, y in all_offsets():
        to = at(a, b, c)
        pltpu.make_async_remote_copy(
            src_ref=give_out.at[to],
            dst_ref=give_in.at[band * ELEMS + me],
            send_sem=send_sems.at[2],
            recv_sem=recv_sems.at[2],
            device_id=(to, (band + y) % BANDS),
            device_id_type=mesh_ids,
        ).start()
    give_in[pl.ds(band * ELEMS + me, 1)] = give_out[pl.ds(me, 1)]
    wait_levels(lw_in, 3, recv_sems)
    scale = 1.0 / (POINTS * BANDS)
    out[1] = total_levels(lw_out, lw_in) * scale

    wait_rows(ask_far, 5, recv_sems, far_peers)
    find_span(jnp.where(near, ask_in[:, 0, :], ask_far[:, 0, :]))
    all_rows = give_in.at[pl.ds(0, BANDS * ELEMS - 1)]
    pltpu.make_async_copy(all_rows, all_rows, recv_sems.at[2]).wait()
    given = give_in[:, 0, :].reshape(BANDS, ELEMS, 128)
    mine[...] = jnp.sum(given, axis=0).T.reshape(SHARE, BANDS, OUT_LEVELS, ELEMS)
    heat = jnp.zeros((2 * OUT_LEVELS, COLS), F)
    for s in range(SHARE):
        heat = heat + jnp.dot(
            jnp.concatenate(pieces(mine[s, band], 2), axis=0).astype(B),
            onehot_span[s * ELEMS : (s + 1) * ELEMS],
            preferred_element_type=F,
        )
    heat = (heat[0:OUT_LEVELS] + heat[OUT_LEVELS:]) * scale
    out[0] = heat * lit[...].astype(F)

    wait_rows(ask_out, 0, send_sems, near_peers)
    wait_rows(tell_out, 1, send_sems, near_peers)
    wait_rows(ask_out, 5, send_sems, far_peers)
    pltpu.make_async_copy(push_in, push_in, send_sems.at[4]).wait()
    pltpu.make_async_copy(all_rows, all_rows, send_sems.at[2]).wait()
    wait_levels(lw_out, 3, send_sems)


def local(
    sw_tau, sw_ssa, lw_tau, lw_source, cosine, surface_albedo, lit_mask, column_map, band_solar, band_table
):
    optics = pltpu.VMEM((LEVELS, POINTS, COLS), B)
    work = pltpu.VMEM((LEVELS, POINTS, COLS), F)
    rows = pltpu.VMEM((ELEMS, 1, 128), F)
    levels = pltpu.VMEM((BANDS, OUT_LEVELS, COLS), F)
    in_hbm = pl.BlockSpec(memory_space=pltpu.HBM)
    in_vmem = pl.BlockSpec(memory_space=pltpu.VMEM)
    return pl.pallas_call(
        kernel,
        out_shape=pltpu.VMEM((2, OUT_LEVELS, COLS), F),
        in_specs=[in_hbm] * 10,
        out_specs=in_vmem,
        scratch_shapes=[
            pltpu.VMEM((1, COLS), F),
            pltpu.VMEM((ALBEDOS, COLS), F),
            pltpu.VMEM((1, COLS), jnp.int32),
            pltpu.VMEM((1, COLS), jnp.int32),
            pltpu.VMEM((1, ALBEDOS), F),
            pltpu.VMEM((1, POINTS), jnp.int32),
            optics, optics, optics, optics, work, work,
            pltpu.VMEM((LEVELS + 1, 8, COLS), F),
            pltpu.VMEM((COLS, COLS), B),
            pltpu.VMEM((COLS, COLS), B),
            pltpu.VMEM((32, COLS), F),
            rows, rows, rows, rows, rows,
            pltpu.VMEM((BANDS * ELEMS, 1, 128), F),
            levels, levels,
            pltpu.VMEM((SHARE, BANDS, OUT_LEVELS, ELEMS), F),
            pltpu.VMEM((SHARE * 32, COLS), B),
            rows,
            pltpu.VMEM((16, COLS), B),
            pltpu.VMEM((len(far_offsets()), 16, COLS), B),
            pltpu.VMEM((COLS, COLS), B),
            pltpu.SemaphoreType.DMA((10,)),
            pltpu.SemaphoreType.DMA((6,)),
            pltpu.SemaphoreType.DMA((6,)),
        ],
        compiler_params=pltpu.CompilerParams(
            collective_id=0, has_side_effects=True, vmem_limit_bytes=(64 * 1024 - 512) * 1024
        ),
    )(
        sw_tau, sw_ssa, lw_tau, lw_source,
        cosine.reshape(1, COLS), surface_albedo, lit_mask.reshape(1, COLS),
        column_map.reshape(1, COLS), band_solar.reshape(1, ALBEDOS), band_table.reshape(1, POINTS),
    )


def solution(mesh):
    placed = (
        P(None, "band", "elem"),
        P(None, "band", "elem"),
        P(None, "band", "elem"),
        P(None, "band", "elem"),
        P("elem"),
        P(None, "elem"),
        P("elem"),
        P("elem"),
        P(),
        P("band"),
    )
    return jax.shard_map(
        local, mesh=mesh, in_specs=placed, out_specs=P(None, "band", "elem"), check_vma=False
    )
```

```python
import functools
import math

import jax
import jax.numpy as jnp
from jax import lax
from jax.experimental import pallas as pl
from jax.experimental.pallas import tpu as pltpu
from jax.sharding import PartitionSpec as P

F = jnp.float32
B = jnp.bfloat16
LOG2E = math.log2(math.e)
DIFFUSE = -1.66 * LOG2E
Z, X, CORES, BANDS = 8, 4, 2, 4
ELEMS = Z * X * CORES
LEVELS, POINTS, COLS, ALBEDOS = 32, 56, 256, 14
SHARE = COLS // ELEMS
OUT_LEVELS = LEVELS // BANDS
NEAR = 3


def elem_offsets():
    offsets = [(a, b, c) for a in range(Z) for b in range(X) for c in range(CORES)][1:]
    return sorted(offsets, key=lambda o: -(min(o[0], Z - o[0]) + min(o[1], X - o[1])))


def far_offsets():
    return [
        (a, b) for a, b, c in elem_offsets() if c == 0 and min(a, Z - a) + min(b, X - b) > NEAR
    ]


def all_offsets():
    offsets = [
        (a, b, c, y) for a in range(Z) for b in range(X) for c in range(CORES) for y in range(BANDS)
    ][1:]
    return sorted(
        offsets, key=lambda o: -(min(o[0], Z - o[0]) + min(o[1], X - o[1]) + min(o[3], BANDS - o[3]))
    )


def iota(shape, dim):
    return lax.broadcasted_iota(jnp.int32, shape, dim)


def over_points(x):
    return jnp.sum(x.reshape(POINTS // 8, 8, x.shape[-1]), axis=0)


def pieces(x, n):
    out = []
    for _ in range(n):
        part = x.astype(B).astype(F)
        out.append(part)
        x = x - part
    return out


def tiled(rows):
    return jnp.concatenate([rows.astype(B)] * SHARE, axis=0)


def spread(parts, onehot):
    picked = [
        lax.dot_general(onehot, rows, (((1,), (1,)), ((), ())), preferred_element_type=F)
        for rows in parts
    ]
    picked = functools.reduce(jnp.add, picked)
    lane_share = iota((ELEMS, 128), 1) // 32
    out = picked[:ELEMS]
    for s in range(1, SHARE):
        out = jnp.where(lane_share == s, picked[s * ELEMS : (s + 1) * ELEMS], out)
    return out


def collect(received, onehot):
    turned = received.T.astype(B)
    out = jnp.zeros((32, COLS), F)
    for s in range(SHARE):
        out = out + jnp.dot(
            turned[s * 32 : (s + 1) * 32],
            onehot[s * ELEMS : (s + 1) * ELEMS],
            preferred_element_type=F,
        )
    return out


def kernel(
    sw_tau, sw_ssa, lw_tau, lw_source, cosine_h, albedo_h, lit_h, map_h, solar_h, table_h,
    out,
    cosine, albedo, lit, column_map, solar, table,
    tau_v, ssa_v, ltau_v, lsrc_v, work_a, work_b, sums, onehot_dyn, onehot_span, params,
    ask_out, ask_in, tell_out, tell_in, give_out, give_in,
    lw_out, lw_in, mine, telling, ask_far, push_out, push_in, slot_of,
    load_sems, send_sems, recv_sems,
):
    me, band = lax.axis_index("elem"), lax.axis_index("band")
    z, x, core = me // (X * CORES), (me // CORES) % X, me % CORES


    def at(a, b, c):
        return ((z + a) % Z) * (X * CORES) + ((x + b) % X) * CORES + (core + c) % CORES

    far = far_offsets()
    push_peers = [at(a, b, 0) for a, b in far]
    far_peers = [at(*o) for o in elem_offsets() if o[:2] in far]
    near_peers = [at(*o) for o in elem_offsets() if o[:2] not in far]
    elem_peers = push_peers + near_peers
    band_peers = [(band + i) % BANDS for i in (2, 1, 3)]
    mesh_ids = pl.DeviceIdType.MESH

    map_load = pltpu.make_async_copy(map_h, column_map, load_sems.at[0])
    map_load.start()
    barrier = pltpu.get_barrier_semaphore()
    for p in elem_peers:
        pl.semaphore_signal(barrier, inc=1, device_id=(p, band), device_id_type=mesh_ids)
    for p in band_peers:
        pl.semaphore_signal(barrier, inc=1, device_id=(me, p), device_id_type=mesh_ids)

    loads = [
        pltpu.make_async_copy(src, dst, load_sems.at[1 + i])
        for i, (src, dst) in enumerate(
            [
                (lw_tau, ltau_v), (lw_source, lsrc_v), (sw_tau, tau_v), (sw_ssa, ssa_v),
                (cosine_h, cosine), (albedo_h, albedo), (lit_h, lit), (solar_h, solar), (table_h, table),
            ]
        )
    ]
    for copy in loads:
        copy.start()

    def send_rows(src, dst, i, peers):
        for p in peers:
            pltpu.make_async_remote_copy(
                src_ref=src.at[p],
                dst_ref=dst.at[me],
                send_sem=send_sems.at[i],
                recv_sem=recv_sems.at[i],
                device_id=(p, band),
                device_id_type=mesh_ids,
            ).start()

    def wait_rows(ref, i, sems, peers):
        rows = ref.at[pl.ds(0, len(peers))]
        pltpu.make_async_copy(rows, rows, sems.at[i]).wait()

    def own_row(src, dst):
        dst[pl.ds(me, 1)] = src[pl.ds(me, 1)]

    def send_levels(src, dst, i):
        for p in band_peers:
            pltpu.make_async_remote_copy(
                src_ref=src.at[p],
                dst_ref=dst.at[band],
                send_sem=send_sems.at[i],
                recv_sem=recv_sems.at[i],
                device_id=(me, p),
                device_id_type=mesh_ids,
            ).start()

    def wait_levels(ref, i, sems):
        part = ref.at[pl.ds(0, BANDS - 1)]
        pltpu.make_async_copy(part, part, sems.at[i]).wait()

    def total_levels(src, dst):
        total = src[band]
        for p in band_peers:
            total = total + dst[p]
        return total

    map_load.wait()
    place = column_map[...]
    owner, slot = place >> 8, place & 255
    turned = jnp.broadcast_to(place.astype(F), (8, COLS)).T[:, 0:1].astype(jnp.int32)
    earlier = ((turned >> 8) == owner) & (iota((COLS, COLS), 0) < iota((COLS, COLS), 1))
    rank = jnp.sum(earlier.astype(F), axis=0, keepdims=True).astype(jnp.int32)
    key = owner + rank * ELEMS
    onehot_dyn[...] = (key == iota((COLS, COLS), 0)).astype(F).astype(B)
    slots = jnp.broadcast_to((turned & 255).astype(F), (COLS, 128)).astype(B)
    asked = jnp.dot(onehot_dyn[...], slots, preferred_element_type=F)
    lane = iota((ELEMS, 128), 1)
    asking = jnp.zeros((ELEMS, 128), F)
    for s in range(SHARE):
        asking = jnp.where(lane == s, asked[s * ELEMS : (s + 1) * ELEMS], asking)
    ask_out[:, 0, :] = asking

    pl.semaphore_wait(barrier, len(elem_peers) + len(band_peers))
    send_rows(ask_out, ask_in, 0, near_peers)

    for copy in loads[4:]:
        copy.wait()
    high, low = pieces(albedo[...], 2)
    params[...] = jnp.zeros((32, COLS), F)
    params[0:ALBEDOS] = high
    params[16 : 16 + ALBEDOS] = low
    first, second, third = pieces(cosine[...], 3)
    params[14:15] = first
    params[15:16] = second
    params[30:31] = third
    telling[...] = tiled(params[...])
    push_out[...] = params[0:16].astype(B)
    slot_of[...] = (slot == iota((COLS, COLS), 0)).astype(F).astype(B)

    for f, (a, b) in enumerate(far):
        pltpu.make_async_remote_copy(
            src_ref=push_out,
            dst_ref=push_in.at[core, far.index(((Z - a) % Z, (X - b) % X))],
            send_sem=send_sems.at[4],
            recv_sem=recv_sems.at[4],
            device_id=(push_peers[f], band),
            device_id_type=mesh_ids,
        ).start()
    own_row(ask_out, ask_in)

    loads[0].wait()
    loads[1].wait()

    def lw_down(k, down):
        planck = lsrc_v[k].astype(F)
        trans = jnp.exp2(ltau_v[k].astype(F) * DIFFUSE)
        emitted = planck - planck * trans
        work_a[k] = trans
        work_b[k] = emitted
        sums[k] = over_points(down)
        return trans * down + emitted

    down = lax.fori_loop(0, LEVELS, lw_down, jnp.zeros((POINTS, COLS), F), unroll=2)
    surface = lsrc_v[LEVELS - 1].astype(F)
    sums[LEVELS] = over_points(down - surface)

    def lw_up(i, up):
        k = LEVELS - 1 - i
        up = work_a[k] * up + work_b[k]
        sums[k] = sums[k] - over_points(up)
        return up

    lax.fori_loop(0, LEVELS, lw_up, surface, unroll=2)

    def layers():
        return jnp.sum(sums[0:LEVELS] - sums[1 : LEVELS + 1], axis=1)

    lw_out[...] = layers().reshape(BANDS, OUT_LEVELS, COLS)
    send_levels(lw_out, lw_in, 3)

    row = iota((ELEMS, 128), 0)
    apart_z, apart_x = ((row >> 3) - z) & (Z - 1), ((row >> 1) - x) & (X - 1)
    near = jnp.minimum(apart_z, Z - apart_z) + jnp.minimum(apart_x, X - apart_x) <= NEAR

    def find_span(asked_of_me):
        asked_of_me = asked_of_me.astype(jnp.int32)
        position = iota((ELEMS, COLS), 1)
        for s in range(SHARE):
            onehot_span[s * ELEMS : (s + 1) * ELEMS] = (
                (asked_of_me[:, s : s + 1] == position).astype(F).astype(B)
            )

    wait_rows(ask_in, 0, recv_sems, near_peers)
    find_span(jnp.where(near, ask_in[:, 0, :], -1.0))
    tell_out[:, 0, :] = spread([telling[...]], onehot_span[...])
    send_rows(tell_out, tell_in, 1, near_peers)
    own_row(tell_out, tell_in)
    send_rows(ask_out, ask_far, 5, far_peers)

    loads[2].wait()
    loads[3].wait()

    def sw_before(i, carry):
        depth, above = carry
        k = LEVELS - 1 - i
        depth = depth + tau_v[i].astype(F) * (1.0 - 0.5 * ssa_v[i].astype(F))
        above = above * jnp.exp2(tau_v[k].astype(F) * DIFFUSE)
        work_a[i] = depth
        work_b[k] = above
        return depth, above

    lax.fori_loop(
        0, LEVELS, sw_before, (jnp.zeros((POINTS, COLS), F), jnp.ones((POINTS, COLS), F)), unroll=2
    )
    diagonal = iota((POINTS, POINTS), 0) == iota((POINTS, POINTS), 1)
    group = jnp.sum(
        jnp.where(diagonal, table[...].astype(F), 0.0), axis=1, keepdims=True
    ).astype(jnp.int32)
    solar_g = jnp.sum(
        jnp.where(iota((POINTS, ALBEDOS), 1) == group, solar[...], 0.0), axis=1, keepdims=True
    )
    lanes = iota((POINTS, 32), 1)
    picks = ((lanes == group) | (lanes == group + 16)).astype(F).astype(B)

    def pick_far(c, found):
        blocks = push_in[c].reshape(len(far) * 16, COLS)
        picked = jnp.dot(blocks, slot_of[...], preferred_element_type=F)
        for f, (a, b) in enumerate(far):
            holder = at(a, b, 0) - core + c
            found = jnp.where(owner == holder, picked[f * 16 : (f + 1) * 16], found)
        return found

    one_core = push_in.at[0]
    pltpu.make_async_copy(one_core, one_core, recv_sems.at[4]).wait()
    pltpu.make_async_remote_copy(
        src_ref=push_in.at[core],
        dst_ref=push_in.at[core],
        send_sem=send_sems.at[6],
        recv_sem=recv_sems.at[6],
        device_id=(at(0, 0, 1), band),
        device_id_type=mesh_ids,
    ).start()
    from_far = pick_far(core, jnp.zeros((16, COLS), F))
    wait_rows(tell_in, 1, recv_sems, near_peers)
    told = collect(jnp.where(near, tell_in[:, 0, :], 0.0), onehot_dyn[...])
    pltpu.make_async_copy(one_core, one_core, recv_sems.at[6]).wait()
    from_far = pick_far(1 - core, from_far)
    told = jnp.concatenate([told[0:16] + from_far, told[16:32]], axis=0)
    cosine_d = told[14:15] + told[15:16] + told[30:31]
    albedo_g = jnp.dot(picks, told.astype(B), preferred_element_type=F)
    slant = -LOG2E / cosine_d
    top = solar_g * cosine_d
    bottom = top * jnp.exp2(work_a[LEVELS - 1] * slant)
    upward = albedo_g * bottom
    sums[0] = over_points(top - upward * work_b[0])
    sums[LEVELS] = over_points(bottom - upward)

    def sw_net(k, carry):
        sums[k] = over_points(top * jnp.exp2(work_a[k - 1] * slant) - upward * work_b[k])
        return carry

    lax.fori_loop(1, LEVELS, sw_net, 0, unroll=31)
    give_out[:, 0, :] = spread([tiled(p) for p in pieces(layers(), 2)], onehot_dyn[...])
    for a, b, c, y in all_offsets():
        to = at(a, b, c)
        pltpu.make_async_remote_copy(
            src_ref=give_out.at[to],
            dst_ref=give_in.at[band * ELEMS + me],
            send_sem=send_sems.at[2],
            recv_sem=recv_sems.at[2],
            device_id=(to, (band + y) % BANDS),
            device_id_type=mesh_ids,
        ).start()
    give_in[pl.ds(band * ELEMS + me, 1)] = give_out[pl.ds(me, 1)]
    wait_levels(lw_in, 3, recv_sems)
    scale = 1.0 / (POINTS * BANDS)
    out[1] = total_levels(lw_out, lw_in) * scale

    wait_rows(ask_far, 5, recv_sems, far_peers)
    find_span(jnp.where(near, ask_in[:, 0, :], ask_far[:, 0, :]))
    all_rows = give_in.at[pl.ds(0, BANDS * ELEMS - 1)]
    pltpu.make_async_copy(all_rows, all_rows, recv_sems.at[2]).wait()
    given = give_in[:, 0, :].reshape(BANDS, ELEMS, 128)
    mine[...] = jnp.sum(given, axis=0).T.reshape(SHARE, BANDS, OUT_LEVELS, ELEMS)
    heat = jnp.zeros((2 * OUT_LEVELS, COLS), F)
    for s in range(SHARE):
        heat = heat + jnp.dot(
            jnp.concatenate(pieces(mine[s, band], 2), axis=0).astype(B),
            onehot_span[s * ELEMS : (s + 1) * ELEMS],
            preferred_element_type=F,
        )
    heat = (heat[0:OUT_LEVELS] + heat[OUT_LEVELS:]) * scale
    out[0] = heat * lit[...].astype(F)

    wait_rows(ask_out, 0, send_sems, near_peers)
    wait_rows(tell_out, 1, send_sems, near_peers)
    wait_rows(ask_out, 5, send_sems, far_peers)
    pltpu.make_async_copy(one_core, one_core, send_sems.at[4]).wait()
    pltpu.make_async_copy(one_core, one_core, send_sems.at[6]).wait()
    pltpu.make_async_copy(all_rows, all_rows, send_sems.at[2]).wait()
    wait_levels(lw_out, 3, send_sems)


def local(
    sw_tau, sw_ssa, lw_tau, lw_source, cosine, surface_albedo, lit_mask, column_map, band_solar, band_table
):
    optics = pltpu.VMEM((LEVELS, POINTS, COLS), B)
    work = pltpu.VMEM((LEVELS, POINTS, COLS), F)
    rows = pltpu.VMEM((ELEMS, 1, 128), F)
    levels = pltpu.VMEM((BANDS, OUT_LEVELS, COLS), F)
    in_hbm = pl.BlockSpec(memory_space=pltpu.HBM)
    in_vmem = pl.BlockSpec(memory_space=pltpu.VMEM)
    return pl.pallas_call(
        kernel,
        out_shape=pltpu.VMEM((2, OUT_LEVELS, COLS), F),
        in_specs=[in_hbm] * 10,
        out_specs=in_vmem,
        scratch_shapes=[
            pltpu.VMEM((1, COLS), F),
            pltpu.VMEM((ALBEDOS, COLS), F),
            pltpu.VMEM((1, COLS), jnp.int32),
            pltpu.VMEM((1, COLS), jnp.int32),
            pltpu.VMEM((1, ALBEDOS), F),
            pltpu.VMEM((1, POINTS), jnp.int32),
            optics, optics, optics, optics, work, work,
            pltpu.VMEM((LEVELS + 1, 8, COLS), F),
            pltpu.VMEM((COLS, COLS), B),
            pltpu.VMEM((COLS, COLS), B),
            pltpu.VMEM((32, COLS), F),
            rows, rows, rows, rows, rows,
            pltpu.VMEM((BANDS * ELEMS, 1, 128), F),
            levels, levels,
            pltpu.VMEM((SHARE, BANDS, OUT_LEVELS, ELEMS), F),
            pltpu.VMEM((SHARE * 32, COLS), B),
            rows,
            pltpu.VMEM((16, COLS), B),
            pltpu.VMEM((CORES, len(far_offsets()), 16, COLS), B),
            pltpu.VMEM((COLS, COLS), B),
            pltpu.SemaphoreType.DMA((10,)),
            pltpu.SemaphoreType.DMA((7,)),
            pltpu.SemaphoreType.DMA((7,)),
        ],
        compiler_params=pltpu.CompilerParams(
            collective_id=0, has_side_effects=True, vmem_limit_bytes=(64 * 1024 - 512) * 1024
        ),
    )(
        sw_tau, sw_ssa, lw_tau, lw_source,
        cosine.reshape(1, COLS), surface_albedo, lit_mask.reshape(1, COLS),
        column_map.reshape(1, COLS), band_solar.reshape(1, ALBEDOS), band_table.reshape(1, POINTS),
    )


def solution(mesh):
    placed = (
        P(None, "band", "elem"),
        P(None, "band", "elem"),
        P(None, "band", "elem"),
        P(None, "band", "elem"),
        P("elem"),
        P(None, "elem"),
        P("elem"),
        P("elem"),
        P(),
        P("band"),
    )
    return jax.shard_map(
        local, mesh=mesh, in_specs=placed, out_specs=P(None, "band", "elem"), check_vma=False
    )
```

```python
import functools
import math

import jax
import jax.numpy as jnp
from jax import lax
from jax.experimental import pallas as pl
from jax.experimental.pallas import tpu as pltpu
from jax.sharding import PartitionSpec as P

F = jnp.float32
B = jnp.bfloat16
LOG2E = math.log2(math.e)
DIFFUSE = -1.66 * LOG2E
Z, X, CORES, BANDS = 8, 4, 2, 4
ELEMS = Z * X * CORES
LEVELS, POINTS, COLS, ALBEDOS = 32, 56, 256, 14
SHARE = COLS // ELEMS
OUT_LEVELS = LEVELS // BANDS
NEAR = 3


def elem_offsets():
    offsets = [(a, b, c) for a in range(Z) for b in range(X) for c in range(CORES)][1:]
    return sorted(offsets, key=lambda o: -(min(o[0], Z - o[0]) + min(o[1], X - o[1])))


def far_offsets():
    return [
        (a, b) for a, b, c in elem_offsets() if c == 0 and min(a, Z - a) + min(b, X - b) > NEAR
    ]


def all_offsets():
    offsets = [
        (a, b, c, y) for a in range(Z) for b in range(X) for c in range(CORES) for y in range(BANDS)
    ][1:]
    return sorted(
        offsets, key=lambda o: -(min(o[0], Z - o[0]) + min(o[1], X - o[1]) + min(o[3], BANDS - o[3]))
    )


def iota(shape, dim):
    return lax.broadcasted_iota(jnp.int32, shape, dim)


def over_points(x):
    return jnp.sum(x.reshape(POINTS // 8, 8, x.shape[-1]), axis=0)


def pieces(x, n):
    out = []
    for _ in range(n):
        part = x.astype(B).astype(F)
        out.append(part)
        x = x - part
    return out


def tiled(rows):
    return jnp.concatenate([rows.astype(B)] * SHARE, axis=0)


def spread(parts, onehot):
    picked = [
        lax.dot_general(onehot, rows, (((1,), (1,)), ((), ())), preferred_element_type=F)
        for rows in parts
    ]
    picked = functools.reduce(jnp.add, picked)
    lane_share = iota((ELEMS, 128), 1) // 32
    out = picked[:ELEMS]
    for s in range(1, SHARE):
        out = jnp.where(lane_share == s, picked[s * ELEMS : (s + 1) * ELEMS], out)
    return out


def collect(received, onehot):
    turned = received.T.astype(B)
    out = jnp.zeros((32, COLS), F)
    for s in range(SHARE):
        out = out + jnp.dot(
            turned[s * 32 : (s + 1) * 32],
            onehot[s * ELEMS : (s + 1) * ELEMS],
            preferred_element_type=F,
        )
    return out


def kernel(
    sw_tau, sw_ssa, lw_tau, lw_source, cosine_h, albedo_h, lit_h, map_h, solar_h, table_h,
    out,
    cosine, albedo, lit, column_map, solar, table,
    tau_v, ssa_v, ltau_v, lsrc_v, work_a, work_b, sums, onehot_dyn, onehot_span, params,
    ask_out, ask_in, tell_out, tell_in, give_out, give_in,
    lw_out, lw_in, mine, telling, ask_far, push_out, push_in, slot_of,
    load_sems, send_sems, recv_sems,
):
    me, band = lax.axis_index("elem"), lax.axis_index("band")
    z, x, core = me // (X * CORES), (me // CORES) % X, me % CORES


    def at(a, b, c):
        return ((z + a) % Z) * (X * CORES) + ((x + b) % X) * CORES + (core + c) % CORES

    far = far_offsets()
    push_peers = [at(a, b, 0) for a, b in far]
    far_peers = [at(*o) for o in elem_offsets() if o[:2] in far]
    near_peers = [at(*o) for o in elem_offsets() if o[:2] not in far]
    elem_peers = push_peers + near_peers
    band_peers = [(band + i) % BANDS for i in (2, 1, 3)]
    mesh_ids = pl.DeviceIdType.MESH

    map_load = pltpu.make_async_copy(map_h, column_map, load_sems.at[0])
    map_load.start()
    barrier = pltpu.get_barrier_semaphore()
    for p in elem_peers:
        pl.semaphore_signal(barrier, inc=1, device_id=(p, band), device_id_type=mesh_ids)
    for p in band_peers:
        pl.semaphore_signal(barrier, inc=1, device_id=(me, p), device_id_type=mesh_ids)

    loads = [
        pltpu.make_async_copy(src, dst, load_sems.at[1 + i])
        for i, (src, dst) in enumerate(
            [
                (lw_tau, ltau_v), (lw_source, lsrc_v), (sw_tau, tau_v), (sw_ssa, ssa_v),
                (cosine_h, cosine), (albedo_h, albedo), (lit_h, lit), (solar_h, solar), (table_h, table),
            ]
        )
    ]
    for copy in loads:
        copy.start()

    def send_rows(src, dst, i, peers):
        for p in peers:
            pltpu.make_async_remote_copy(
                src_ref=src.at[p],
                dst_ref=dst.at[me],
                send_sem=send_sems.at[i],
                recv_sem=recv_sems.at[i],
                device_id=(p, band),
                device_id_type=mesh_ids,
            ).start()

    def wait_rows(ref, i, sems, peers):
        rows = ref.at[pl.ds(0, len(peers))]
        pltpu.make_async_copy(rows, rows, sems.at[i]).wait()

    def own_row(src, dst):
        dst[pl.ds(me, 1)] = src[pl.ds(me, 1)]

    def send_levels(src, dst, i):
        for p in band_peers:
            pltpu.make_async_remote_copy(
                src_ref=src.at[p],
                dst_ref=dst.at[band],
                send_sem=send_sems.at[i],
                recv_sem=recv_sems.at[i],
                device_id=(me, p),
                device_id_type=mesh_ids,
            ).start()

    def wait_levels(ref, i, sems):
        part = ref.at[pl.ds(0, BANDS - 1)]
        pltpu.make_async_copy(part, part, sems.at[i]).wait()

    def total_levels(src, dst):
        total = src[band]
        for p in band_peers:
            total = total + dst[p]
        return total

    map_load.wait()
    place = column_map[...]
    owner, slot = place >> 8, place & 255
    turned = jnp.broadcast_to(place.astype(F), (8, COLS)).T[:, 0:1].astype(jnp.int32)
    earlier = ((turned >> 8) == owner) & (iota((COLS, COLS), 0) < iota((COLS, COLS), 1))
    rank = jnp.sum(earlier.astype(F), axis=0, keepdims=True).astype(jnp.int32)
    key = owner + rank * ELEMS
    onehot_dyn[...] = (key == iota((COLS, COLS), 0)).astype(F).astype(B)
    slots = jnp.broadcast_to((turned & 255).astype(F), (COLS, 128)).astype(B)
    asked = jnp.dot(onehot_dyn[...], slots, preferred_element_type=F)
    lane = iota((ELEMS, 128), 1)
    asking = jnp.zeros((ELEMS, 128), F)
    for s in range(SHARE):
        asking = jnp.where(lane == s, asked[s * ELEMS : (s + 1) * ELEMS], asking)
    ask_out[:, 0, :] = asking

    pl.semaphore_wait(barrier, len(elem_peers) + len(band_peers))
    send_rows(ask_out, ask_in, 0, near_peers)

    for copy in loads[4:]:
        copy.wait()
    high, low = pieces(albedo[...], 2)
    params[...] = jnp.zeros((32, COLS), F)
    params[0:ALBEDOS] = high
    params[16 : 16 + ALBEDOS] = low
    first, second, third = pieces(cosine[...], 3)
    params[14:15] = first
    params[15:16] = second
    params[30:31] = third
    telling[...] = tiled(params[...])
    push_out[...] = params[0:16].astype(B)
    slot_of[...] = (slot == iota((COLS, COLS), 0)).astype(F).astype(B)

    for f, (a, b) in enumerate(far):
        pltpu.make_async_remote_copy(
            src_ref=push_out,
            dst_ref=push_in.at[core, far.index(((Z - a) % Z, (X - b) % X))],
            send_sem=send_sems.at[4],
            recv_sem=recv_sems.at[4],
            device_id=(push_peers[f], band),
            device_id_type=mesh_ids,
        ).start()
    own_row(ask_out, ask_in)

    loads[0].wait()
    loads[1].wait()

    def lw_down(k, down):
        planck = lsrc_v[k].astype(F)
        trans = jnp.exp2(ltau_v[k].astype(F) * DIFFUSE)
        emitted = planck - planck * trans
        work_a[k] = trans
        work_b[k] = emitted
        sums[k] = over_points(down)
        return trans * down + emitted

    down = lax.fori_loop(0, LEVELS, lw_down, jnp.zeros((POINTS, COLS), F), unroll=2)
    surface = lsrc_v[LEVELS - 1].astype(F)
    sums[LEVELS] = over_points(down - surface)

    def lw_up(i, up):
        k = LEVELS - 1 - i
        up = work_a[k] * up + work_b[k]
        sums[k] = sums[k] - over_points(up)
        return up

    lax.fori_loop(0, LEVELS, lw_up, surface, unroll=2)

    def layers():
        return jnp.sum(sums[0:LEVELS] - sums[1 : LEVELS + 1], axis=1)

    lw_out[...] = layers().reshape(BANDS, OUT_LEVELS, COLS)
    send_levels(lw_out, lw_in, 3)

    row = iota((ELEMS, 128), 0)
    apart_z, apart_x = ((row >> 3) - z) & (Z - 1), ((row >> 1) - x) & (X - 1)
    near = jnp.minimum(apart_z, Z - apart_z) + jnp.minimum(apart_x, X - apart_x) <= NEAR

    def find_span(asked_of_me):
        asked_of_me = asked_of_me.astype(jnp.int32)
        position = iota((ELEMS, COLS), 1)
        for s in range(SHARE):
            onehot_span[s * ELEMS : (s + 1) * ELEMS] = (
                (asked_of_me[:, s : s + 1] == position).astype(F).astype(B)
            )

    wait_rows(ask_in, 0, recv_sems, near_peers)
    find_span(jnp.where(near, ask_in[:, 0, :], -1.0))
    tell_out[:, 0, :] = spread([telling[...]], onehot_span[...])
    send_rows(tell_out, tell_in, 1, near_peers)
    own_row(tell_out, tell_in)
    send_rows(ask_out, ask_far, 5, far_peers)

    loads[2].wait()
    loads[3].wait()

    def sw_before(i, carry):
        depth, above = carry
        k = LEVELS - 1 - i
        depth = depth + tau_v[i].astype(F) * (1.0 - 0.5 * ssa_v[i].astype(F))
        above = above * jnp.exp2(tau_v[k].astype(F) * DIFFUSE)
        work_a[i] = depth
        work_b[k] = above
        return depth, above

    lax.fori_loop(
        0, LEVELS, sw_before, (jnp.zeros((POINTS, COLS), F), jnp.ones((POINTS, COLS), F)), unroll=2
    )
    diagonal = iota((POINTS, POINTS), 0) == iota((POINTS, POINTS), 1)
    group = jnp.sum(
        jnp.where(diagonal, table[...].astype(F), 0.0), axis=1, keepdims=True
    ).astype(jnp.int32)
    solar_g = jnp.sum(
        jnp.where(iota((POINTS, ALBEDOS), 1) == group, solar[...], 0.0), axis=1, keepdims=True
    )
    lanes = iota((POINTS, 32), 1)
    picks = ((lanes == group) | (lanes == group + 16)).astype(F).astype(B)

    def pick_far(c, found):
        blocks = push_in[c].reshape(len(far) * 16, COLS)
        picked = jnp.dot(blocks, slot_of[...], preferred_element_type=F)
        for f, (a, b) in enumerate(far):
            holder = at(a, b, 0) - core + c
            found = jnp.where(owner == holder, picked[f * 16 : (f + 1) * 16], found)
        return found

    one_core = push_in.at[0]
    pltpu.make_async_copy(one_core, one_core, recv_sems.at[4]).wait()
    pltpu.make_async_remote_copy(
        src_ref=push_in.at[core],
        dst_ref=push_in.at[core],
        send_sem=send_sems.at[6],
        recv_sem=recv_sems.at[6],
        device_id=(at(0, 0, 1), band),
        device_id_type=mesh_ids,
    ).start()
    from_far = pick_far(core, jnp.zeros((16, COLS), F))
    pltpu.make_async_copy(one_core, one_core, recv_sems.at[6]).wait()
    from_far = pick_far(1 - core, from_far)
    wait_rows(tell_in, 1, recv_sems, near_peers)
    told = collect(jnp.where(near, tell_in[:, 0, :], 0.0), onehot_dyn[...])
    told = jnp.concatenate([told[0:16] + from_far, told[16:32]], axis=0)
    cosine_d = told[14:15] + told[15:16] + told[30:31]
    albedo_g = jnp.dot(picks, told.astype(B), preferred_element_type=F)
    slant = -LOG2E / cosine_d
    top = solar_g * cosine_d
    bottom = top * jnp.exp2(work_a[LEVELS - 1] * slant)
    upward = albedo_g * bottom
    sums[0] = over_points(top - upward * work_b[0])
    sums[LEVELS] = over_points(bottom - upward)

    def sw_net(k, carry):
        sums[k] = over_points(top * jnp.exp2(work_a[k - 1] * slant) - upward * work_b[k])
        return carry

    lax.fori_loop(1, LEVELS, sw_net, 0, unroll=31)
    give_out[:, 0, :] = spread([tiled(p) for p in pieces(layers(), 2)], onehot_dyn[...])
    for a, b, c, y in all_offsets():
        to = at(a, b, c)
        pltpu.make_async_remote_copy(
            src_ref=give_out.at[to],
            dst_ref=give_in.at[band * ELEMS + me],
            send_sem=send_sems.at[2],
            recv_sem=recv_sems.at[2],
            device_id=(to, (band + y) % BANDS),
            device_id_type=mesh_ids,
        ).start()
    give_in[pl.ds(band * ELEMS + me, 1)] = give_out[pl.ds(me, 1)]
    wait_levels(lw_in, 3, recv_sems)
    scale = 1.0 / (POINTS * BANDS)
    out[1] = total_levels(lw_out, lw_in) * scale

    wait_rows(ask_far, 5, recv_sems, far_peers)
    find_span(jnp.where(near, ask_in[:, 0, :], ask_far[:, 0, :]))
    all_rows = give_in.at[pl.ds(0, BANDS * ELEMS - 1)]
    pltpu.make_async_copy(all_rows, all_rows, recv_sems.at[2]).wait()
    given = give_in[:, 0, :].reshape(BANDS, ELEMS, 128)
    mine[...] = jnp.sum(given, axis=0).T.reshape(SHARE, BANDS, OUT_LEVELS, ELEMS)
    heat = jnp.zeros((2 * OUT_LEVELS, COLS), F)
    for s in range(SHARE):
        heat = heat + jnp.dot(
            jnp.concatenate(pieces(mine[s, band], 2), axis=0).astype(B),
            onehot_span[s * ELEMS : (s + 1) * ELEMS],
            preferred_element_type=F,
        )
    heat = (heat[0:OUT_LEVELS] + heat[OUT_LEVELS:]) * scale
    out[0] = heat * lit[...].astype(F)

    wait_rows(ask_out, 0, send_sems, near_peers)
    wait_rows(tell_out, 1, send_sems, near_peers)
    wait_rows(ask_out, 5, send_sems, far_peers)
    pltpu.make_async_copy(one_core, one_core, send_sems.at[4]).wait()
    pltpu.make_async_copy(one_core, one_core, send_sems.at[6]).wait()
    pltpu.make_async_copy(all_rows, all_rows, send_sems.at[2]).wait()
    wait_levels(lw_out, 3, send_sems)


def local(
    sw_tau, sw_ssa, lw_tau, lw_source, cosine, surface_albedo, lit_mask, column_map, band_solar, band_table
):
    optics = pltpu.VMEM((LEVELS, POINTS, COLS), B)
    work = pltpu.VMEM((LEVELS, POINTS, COLS), F)
    rows = pltpu.VMEM((ELEMS, 1, 128), F)
    levels = pltpu.VMEM((BANDS, OUT_LEVELS, COLS), F)
    in_hbm = pl.BlockSpec(memory_space=pltpu.HBM)
    in_vmem = pl.BlockSpec(memory_space=pltpu.VMEM)
    return pl.pallas_call(
        kernel,
        out_shape=pltpu.VMEM((2, OUT_LEVELS, COLS), F),
        in_specs=[in_hbm] * 10,
        out_specs=in_vmem,
        scratch_shapes=[
            pltpu.VMEM((1, COLS), F),
            pltpu.VMEM((ALBEDOS, COLS), F),
            pltpu.VMEM((1, COLS), jnp.int32),
            pltpu.VMEM((1, COLS), jnp.int32),
            pltpu.VMEM((1, ALBEDOS), F),
            pltpu.VMEM((1, POINTS), jnp.int32),
            optics, optics, optics, optics, work, work,
            pltpu.VMEM((LEVELS + 1, 8, COLS), F),
            pltpu.VMEM((COLS, COLS), B),
            pltpu.VMEM((COLS, COLS), B),
            pltpu.VMEM((32, COLS), F),
            rows, rows, rows, rows, rows,
            pltpu.VMEM((BANDS * ELEMS, 1, 128), F),
            levels, levels,
            pltpu.VMEM((SHARE, BANDS, OUT_LEVELS, ELEMS), F),
            pltpu.VMEM((SHARE * 32, COLS), B),
            rows,
            pltpu.VMEM((16, COLS), B),
            pltpu.VMEM((CORES, len(far_offsets()), 16, COLS), B),
            pltpu.VMEM((COLS, COLS), B),
            pltpu.SemaphoreType.DMA((10,)),
            pltpu.SemaphoreType.DMA((7,)),
            pltpu.SemaphoreType.DMA((7,)),
        ],
        compiler_params=pltpu.CompilerParams(
            collective_id=0, has_side_effects=True, vmem_limit_bytes=(64 * 1024 - 512) * 1024
        ),
    )(
        sw_tau, sw_ssa, lw_tau, lw_source,
        cosine.reshape(1, COLS), surface_albedo, lit_mask.reshape(1, COLS),
        column_map.reshape(1, COLS), band_solar.reshape(1, ALBEDOS), band_table.reshape(1, POINTS),
    )


def solution(mesh):
    placed = (
        P(None, "band", "elem"),
        P(None, "band", "elem"),
        P(None, "band", "elem"),
        P(None, "band", "elem"),
        P("elem"),
        P(None, "elem"),
        P("elem"),
        P("elem"),
        P(),
        P("band"),
    )
    return jax.shard_map(
        local, mesh=mesh, in_specs=placed, out_specs=P(None, "band", "elem"), check_vma=False
    )
```

```python
import functools
import math

import jax
import jax.numpy as jnp
from jax import lax
from jax.experimental import pallas as pl
from jax.experimental.pallas import tpu as pltpu
from jax.sharding import PartitionSpec as P

F = jnp.float32
B = jnp.bfloat16
LOG2E = math.log2(math.e)
DIFFUSE = -1.66 * LOG2E
Z, X, CORES, BANDS = 8, 4, 2, 4
ELEMS = Z * X * CORES
LEVELS, POINTS, COLS, ALBEDOS = 32, 56, 256, 14
SHARE = COLS // ELEMS
OUT_LEVELS = LEVELS // BANDS
NEAR = 3


def elem_offsets():
    offsets = [(a, b, c) for a in range(Z) for b in range(X) for c in range(CORES)][1:]
    return sorted(offsets, key=lambda o: -(min(o[0], Z - o[0]) + min(o[1], X - o[1])))


def far_offsets():
    return [
        (a, b) for a, b, c in elem_offsets() if c == 0 and min(a, Z - a) + min(b, X - b) > NEAR
    ]


def all_offsets():
    offsets = [
        (a, b, c, y) for a in range(Z) for b in range(X) for c in range(CORES) for y in range(BANDS)
    ][1:]
    return sorted(
        offsets, key=lambda o: -(min(o[0], Z - o[0]) + min(o[1], X - o[1]) + min(o[3], BANDS - o[3]))
    )


def iota(shape, dim):
    return lax.broadcasted_iota(jnp.int32, shape, dim)


def over_points(x):
    return jnp.sum(x.reshape(POINTS // 8, 8, x.shape[-1]), axis=0)


def pieces(x, n):
    out = []
    for _ in range(n):
        part = x.astype(B).astype(F)
        out.append(part)
        x = x - part
    return out


def tiled(rows):
    return jnp.concatenate([rows.astype(B)] * SHARE, axis=0)


def spread(parts, onehot):
    picked = [
        lax.dot_general(onehot, rows, (((1,), (1,)), ((), ())), preferred_element_type=F)
        for rows in parts
    ]
    picked = functools.reduce(jnp.add, picked)
    lane_share = iota((ELEMS, 128), 1) // 32
    out = picked[:ELEMS]
    for s in range(1, SHARE):
        out = jnp.where(lane_share == s, picked[s * ELEMS : (s + 1) * ELEMS], out)
    return out


def collect(received, onehot):
    turned = received.T.astype(B)
    out = jnp.zeros((32, COLS), F)
    for s in range(SHARE):
        out = out + jnp.dot(
            turned[s * 32 : (s + 1) * 32],
            onehot[s * ELEMS : (s + 1) * ELEMS],
            preferred_element_type=F,
        )
    return out


def kernel(
    sw_tau, sw_ssa, lw_tau, lw_source, cosine_h, albedo_h, lit_h, map_h, solar_h, table_h,
    out,
    cosine, albedo, lit, column_map, solar, table,
    tau_v, ssa_v, ltau_v, lsrc_v, work_a, work_b, sums, onehot_dyn, onehot_span, params,
    ask_out, ask_in, tell_out, tell_in, give_out, give_in,
    lw_out, lw_in, mine, telling, ask_far, push_out, push_in, slot_of,
    load_sems, send_sems, recv_sems,
):
    me, band = lax.axis_index("elem"), lax.axis_index("band")
    z, x, core = me // (X * CORES), (me // CORES) % X, me % CORES


    def at(a, b, c):
        return ((z + a) % Z) * (X * CORES) + ((x + b) % X) * CORES + (core + c) % CORES

    far = far_offsets()
    push_peers = [at(a, b, 0) for a, b in far]
    far_peers = [at(*o) for o in elem_offsets() if o[:2] in far]
    near_peers = [at(*o) for o in elem_offsets() if o[:2] not in far]
    elem_peers = push_peers + near_peers
    band_peers = [(band + i) % BANDS for i in (2, 1, 3)]
    mesh_ids = pl.DeviceIdType.MESH

    map_load = pltpu.make_async_copy(map_h, column_map, load_sems.at[0])
    map_load.start()
    barrier = pltpu.get_barrier_semaphore()
    for p in elem_peers:
        pl.semaphore_signal(barrier, inc=1, device_id=(p, band), device_id_type=mesh_ids)
    for p in band_peers:
        pl.semaphore_signal(barrier, inc=1, device_id=(me, p), device_id_type=mesh_ids)

    loads = [
        pltpu.make_async_copy(src, dst, load_sems.at[1 + i])
        for i, (src, dst) in enumerate(
            [
                (lw_tau, ltau_v), (lw_source, lsrc_v), (sw_tau, tau_v), (sw_ssa, ssa_v),
                (cosine_h, cosine), (albedo_h, albedo), (lit_h, lit), (solar_h, solar), (table_h, table),
            ]
        )
    ]
    for copy in loads:
        copy.start()

    def send_rows(src, dst, i, peers):
        for p in peers:
            pltpu.make_async_remote_copy(
                src_ref=src.at[p],
                dst_ref=dst.at[me],
                send_sem=send_sems.at[i],
                recv_sem=recv_sems.at[i],
                device_id=(p, band),
                device_id_type=mesh_ids,
            ).start()

    def wait_rows(ref, i, sems, peers):
        rows = ref.at[pl.ds(0, len(peers))]
        pltpu.make_async_copy(rows, rows, sems.at[i]).wait()

    def own_row(src, dst):
        dst[pl.ds(me, 1)] = src[pl.ds(me, 1)]

    def send_levels(src, dst, i):
        for p in band_peers:
            pltpu.make_async_remote_copy(
                src_ref=src.at[p],
                dst_ref=dst.at[band],
                send_sem=send_sems.at[i],
                recv_sem=recv_sems.at[i],
                device_id=(me, p),
                device_id_type=mesh_ids,
            ).start()

    def wait_levels(ref, i, sems):
        part = ref.at[pl.ds(0, BANDS - 1)]
        pltpu.make_async_copy(part, part, sems.at[i]).wait()

    def total_levels(src, dst):
        total = src[band]
        for p in band_peers:
            total = total + dst[p]
        return total

    map_load.wait()
    place = column_map[...]
    owner, slot = place >> 8, place & 255
    turned = jnp.broadcast_to(place.astype(F), (8, COLS)).T[:, 0:1].astype(jnp.int32)
    earlier = ((turned >> 8) == owner) & (iota((COLS, COLS), 0) < iota((COLS, COLS), 1))
    rank = jnp.sum(earlier.astype(F), axis=0, keepdims=True).astype(jnp.int32)
    key = owner + rank * ELEMS
    onehot_dyn[...] = (key == iota((COLS, COLS), 0)).astype(F).astype(B)
    slots = jnp.broadcast_to((turned & 255).astype(F), (COLS, 128)).astype(B)
    asked = jnp.dot(onehot_dyn[...], slots, preferred_element_type=F)
    lane = iota((ELEMS, 128), 1)
    asking = jnp.zeros((ELEMS, 128), F)
    for s in range(SHARE):
        asking = jnp.where(lane == s, asked[s * ELEMS : (s + 1) * ELEMS], asking)
    ask_out[:, 0, :] = asking

    pl.semaphore_wait(barrier, len(elem_peers) + len(band_peers))
    send_rows(ask_out, ask_in, 0, near_peers)

    for copy in loads[4:]:
        copy.wait()
    high, low = pieces(albedo[...], 2)
    params[...] = jnp.zeros((32, COLS), F)
    params[0:ALBEDOS] = high
    params[16 : 16 + ALBEDOS] = low
    first, second, third = pieces(cosine[...], 3)
    params[14:15] = first
    params[15:16] = second
    params[30:31] = third
    telling[...] = tiled(params[...])
    push_out[...] = params[0:16].astype(B)
    slot_of[...] = (slot == iota((COLS, COLS), 0)).astype(F).astype(B)

    for f, (a, b) in enumerate(far):
        pltpu.make_async_remote_copy(
            src_ref=push_out,
            dst_ref=push_in.at[core, far.index(((Z - a) % Z, (X - b) % X))],
            send_sem=send_sems.at[4],
            recv_sem=recv_sems.at[4],
            device_id=(push_peers[f], band),
            device_id_type=mesh_ids,
        ).start()
    own_row(ask_out, ask_in)

    loads[0].wait()
    loads[1].wait()

    def lw_down(k, down):
        planck = lsrc_v[k].astype(F)
        trans = jnp.exp2(ltau_v[k].astype(F) * DIFFUSE)
        emitted = planck - planck * trans
        work_a[k] = trans
        work_b[k] = emitted
        sums[k] = over_points(down)
        return trans * down + emitted

    down = lax.fori_loop(0, LEVELS, lw_down, jnp.zeros((POINTS, COLS), F), unroll=2)
    surface = lsrc_v[LEVELS - 1].astype(F)
    sums[LEVELS] = over_points(down - surface)

    def lw_up(i, up):
        k = LEVELS - 1 - i
        up = work_a[k] * up + work_b[k]
        sums[k] = sums[k] - over_points(up)
        return up

    lax.fori_loop(0, LEVELS, lw_up, surface, unroll=2)

    def layers():
        return jnp.sum(sums[0:LEVELS] - sums[1 : LEVELS + 1], axis=1)

    lw_out[...] = layers().reshape(BANDS, OUT_LEVELS, COLS)
    send_levels(lw_out, lw_in, 3)

    row = iota((ELEMS, 128), 0)
    apart_z, apart_x = ((row >> 3) - z) & (Z - 1), ((row >> 1) - x) & (X - 1)
    near = jnp.minimum(apart_z, Z - apart_z) + jnp.minimum(apart_x, X - apart_x) <= NEAR

    def find_span(asked_of_me):
        asked_of_me = asked_of_me.astype(jnp.int32)
        position = iota((ELEMS, COLS), 1)
        for s in range(SHARE):
            onehot_span[s * ELEMS : (s + 1) * ELEMS] = (
                (asked_of_me[:, s : s + 1] == position).astype(F).astype(B)
            )

    wait_rows(ask_in, 0, recv_sems, near_peers)
    find_span(jnp.where(near, ask_in[:, 0, :], -1.0))
    tell_out[:, 0, :] = spread([telling[...]], onehot_span[...])
    send_rows(tell_out, tell_in, 1, near_peers)
    own_row(tell_out, tell_in)
    send_rows(ask_out, ask_far, 5, far_peers)

    loads[2].wait()
    loads[3].wait()

    def sw_before(i, carry):
        depth, above = carry
        k = LEVELS - 1 - i
        depth = depth + tau_v[i].astype(F) * (1.0 - 0.5 * ssa_v[i].astype(F))
        above = above * jnp.exp2(tau_v[k].astype(F) * DIFFUSE)
        work_a[i] = depth
        work_b[k] = above
        return depth, above

    lax.fori_loop(
        0, LEVELS, sw_before, (jnp.zeros((POINTS, COLS), F), jnp.ones((POINTS, COLS), F)), unroll=2
    )
    diagonal = iota((POINTS, POINTS), 0) == iota((POINTS, POINTS), 1)
    group = jnp.sum(
        jnp.where(diagonal, table[...].astype(F), 0.0), axis=1, keepdims=True
    ).astype(jnp.int32)
    solar_g = jnp.sum(
        jnp.where(iota((POINTS, ALBEDOS), 1) == group, solar[...], 0.0), axis=1, keepdims=True
    )
    lanes = iota((POINTS, 32), 1)
    picks = ((lanes == group) | (lanes == group + 16)).astype(F).astype(B)

    def pick_far(c, found):
        blocks = push_in[c].reshape(len(far) * 16, COLS)
        picked = jnp.dot(blocks, slot_of[...], preferred_element_type=F)
        for f, (a, b) in enumerate(far):
            holder = at(a, b, 0) - core + c
            found = jnp.where(owner == holder, picked[f * 16 : (f + 1) * 16], found)
        return found

    one_core = push_in.at[0]
    pltpu.make_async_copy(one_core, one_core, recv_sems.at[4]).wait()
    pltpu.make_async_remote_copy(
        src_ref=push_in.at[core],
        dst_ref=push_in.at[core],
        send_sem=send_sems.at[6],
        recv_sem=recv_sems.at[6],
        device_id=(at(0, 0, 1), band),
        device_id_type=mesh_ids,
    ).start()
    from_far = pick_far(core, jnp.zeros((16, COLS), F))
    pltpu.make_async_copy(one_core, one_core, recv_sems.at[6]).wait()
    from_far = pick_far(1 - core, from_far)
    wait_rows(tell_in, 1, recv_sems, near_peers)
    told = collect(jnp.where(near, tell_in[:, 0, :], 0.0), onehot_dyn[...])
    told = jnp.concatenate([told[0:16] + from_far, told[16:32]], axis=0)
    cosine_d = told[14:15] + told[15:16] + told[30:31]
    albedo_g = jnp.dot(picks, told.astype(B), preferred_element_type=F)
    slant = -LOG2E / cosine_d
    top = solar_g * cosine_d
    bottom = top * jnp.exp2(work_a[LEVELS - 1] * slant)
    upward = albedo_g * bottom
    below = over_points(bottom - upward)
    heats = [None] * LEVELS
    for k in range(LEVELS - 1, -1, -1):
        direct = top * jnp.exp2(work_a[k - 1] * slant) if k else top
        here = over_points(direct - upward * work_b[k])
        heats[k] = jnp.sum(here - below, axis=0, keepdims=True)
        below = here
    give_out[:, 0, :] = spread([tiled(p) for p in pieces(jnp.concatenate(heats, axis=0), 2)], onehot_dyn[...])
    for a, b, c, y in all_offsets():
        to = at(a, b, c)
        pltpu.make_async_remote_copy(
            src_ref=give_out.at[to],
            dst_ref=give_in.at[band * ELEMS + me],
            send_sem=send_sems.at[2],
            recv_sem=recv_sems.at[2],
            device_id=(to, (band + y) % BANDS),
            device_id_type=mesh_ids,
        ).start()
    give_in[pl.ds(band * ELEMS + me, 1)] = give_out[pl.ds(me, 1)]
    wait_levels(lw_in, 3, recv_sems)
    scale = 1.0 / (POINTS * BANDS)
    out[1] = total_levels(lw_out, lw_in) * scale

    wait_rows(ask_far, 5, recv_sems, far_peers)
    find_span(jnp.where(near, ask_in[:, 0, :], ask_far[:, 0, :]))
    all_rows = give_in.at[pl.ds(0, BANDS * ELEMS - 1)]
    pltpu.make_async_copy(all_rows, all_rows, recv_sems.at[2]).wait()
    given = give_in[:, 0, :].reshape(BANDS, ELEMS, 128)
    mine[...] = jnp.sum(given, axis=0).T.reshape(SHARE, BANDS, OUT_LEVELS, ELEMS)
    heat = jnp.zeros((2 * OUT_LEVELS, COLS), F)
    for s in range(SHARE):
        heat = heat + jnp.dot(
            jnp.concatenate(pieces(mine[s, band], 2), axis=0).astype(B),
            onehot_span[s * ELEMS : (s + 1) * ELEMS],
            preferred_element_type=F,
        )
    heat = (heat[0:OUT_LEVELS] + heat[OUT_LEVELS:]) * scale
    out[0] = heat * lit[...].astype(F)

    wait_rows(ask_out, 0, send_sems, near_peers)
    wait_rows(tell_out, 1, send_sems, near_peers)
    wait_rows(ask_out, 5, send_sems, far_peers)
    pltpu.make_async_copy(one_core, one_core, send_sems.at[4]).wait()
    pltpu.make_async_copy(one_core, one_core, send_sems.at[6]).wait()
    pltpu.make_async_copy(all_rows, all_rows, send_sems.at[2]).wait()
    wait_levels(lw_out, 3, send_sems)


def local(
    sw_tau, sw_ssa, lw_tau, lw_source, cosine, surface_albedo, lit_mask, column_map, band_solar, band_table
):
    optics = pltpu.VMEM((LEVELS, POINTS, COLS), B)
    work = pltpu.VMEM((LEVELS, POINTS, COLS), F)
    rows = pltpu.VMEM((ELEMS, 1, 128), F)
    levels = pltpu.VMEM((BANDS, OUT_LEVELS, COLS), F)
    in_hbm = pl.BlockSpec(memory_space=pltpu.HBM)
    in_vmem = pl.BlockSpec(memory_space=pltpu.VMEM)
    return pl.pallas_call(
        kernel,
        out_shape=pltpu.VMEM((2, OUT_LEVELS, COLS), F),
        in_specs=[in_hbm] * 10,
        out_specs=in_vmem,
        scratch_shapes=[
            pltpu.VMEM((1, COLS), F),
            pltpu.VMEM((ALBEDOS, COLS), F),
            pltpu.VMEM((1, COLS), jnp.int32),
            pltpu.VMEM((1, COLS), jnp.int32),
            pltpu.VMEM((1, ALBEDOS), F),
            pltpu.VMEM((1, POINTS), jnp.int32),
            optics, optics, optics, optics, work, work,
            pltpu.VMEM((LEVELS + 1, 8, COLS), F),
            pltpu.VMEM((COLS, COLS), B),
            pltpu.VMEM((COLS, COLS), B),
            pltpu.VMEM((32, COLS), F),
            rows, rows, rows, rows, rows,
            pltpu.VMEM((BANDS * ELEMS, 1, 128), F),
            levels, levels,
            pltpu.VMEM((SHARE, BANDS, OUT_LEVELS, ELEMS), F),
            pltpu.VMEM((SHARE * 32, COLS), B),
            rows,
            pltpu.VMEM((16, COLS), B),
            pltpu.VMEM((CORES, len(far_offsets()), 16, COLS), B),
            pltpu.VMEM((COLS, COLS), B),
            pltpu.SemaphoreType.DMA((10,)),
            pltpu.SemaphoreType.DMA((7,)),
            pltpu.SemaphoreType.DMA((7,)),
        ],
        compiler_params=pltpu.CompilerParams(
            collective_id=0, has_side_effects=True, vmem_limit_bytes=(64 * 1024 - 512) * 1024
        ),
    )(
        sw_tau, sw_ssa, lw_tau, lw_source,
        cosine.reshape(1, COLS), surface_albedo, lit_mask.reshape(1, COLS),
        column_map.reshape(1, COLS), band_solar.reshape(1, ALBEDOS), band_table.reshape(1, POINTS),
    )


def solution(mesh):
    placed = (
        P(None, "band", "elem"),
        P(None, "band", "elem"),
        P(None, "band", "elem"),
        P(None, "band", "elem"),
        P("elem"),
        P(None, "elem"),
        P("elem"),
        P("elem"),
        P(),
        P("band"),
    )
    return jax.shard_map(
        local, mesh=mesh, in_specs=placed, out_specs=P(None, "band", "elem"), check_vma=False
    )
```
